128 devices in a mesh: dp: 32 (over z, y, core), blk: 4 (over x).
Axes of the slice: x: 4, y: 4, z: 4, core: 2. Of those that a mesh axis runs over, the one named last changes fastest.
Arguments:
- queries: bfloat16 [16384, 4096], P(('dp', 'blk')), may hold values from -24 to 24
- passages: bfloat16 [98304, 4096], P(('dp', 'blk')), may hold values from -6 to 6
- neg_table: bfloat16 [32768, 4096], P('dp'), may hold values from -6 to 6
- neg_ids: int32 [16384, 16], P(('dp', 'blk')), may hold values from 0 to 32767, as said below
- counts: int32 [16384], P(('dp', 'blk')), may hold values from 1 to 16
- neg_home: int32 [32768], replicated, may hold values from 0 to 32767, as said below
Outputs:
- loss: float32 [16384], P(('dp', 'blk'))
- grad_queries: bfloat16 [16384, 4096], P(('dp', 'blk'))
- grad_passages: bfloat16 [98304, 4096], P(('dp', 'blk'))
The draws below stay inside these ranges and needn't reach their ends.
Inputs may be any that keep to these rules, and one draw needn't show every extreme that they name: `neg_ids`: within each device's 128 queries, the slots (query, k) taken in order in groups of 64 name passages held by one index of dp each, a different index for each group. `neg_home`: each index row is named once.
All inputs are finite; a program needn't handle non-finite values.
Results may differ from the reference program's by a relative error of at most 0.0065.
Values may be sent and summed in bfloat16 or wider, within the bound.
A program may use at most 192 MiB of HBM per device.

```python
import jax
import jax.numpy as jnp
from jax import lax

D = 4096
QD = 128
PD = 768
K = 16
NEG_DEV = 1024
QUERIES = 16384
PASSAGES = 98304
CAP = 64
N_DP = 32
N_BLK = 4


def home_rows(key):
    return jax.random.permutation(key, NEG_DEV * N_DP).astype(jnp.int32)


def id_rows(key):
    home = home_rows(key)
    inner = jax.random.fold_in(key, 5)
    total = NEG_DEV * N_DP
    inverse = jnp.zeros((total,), jnp.int32).at[home].set(jnp.arange(total, dtype=jnp.int32))
    devices = QUERIES // QD
    keys = jax.random.split(jax.random.fold_in(inner, 1), devices)

    def owner_order(one_key):
        return jax.random.permutation(one_key, N_DP).astype(jnp.int32)
    owners = jax.vmap(owner_order)(keys)
    owner_slot = jnp.repeat(owners, CAP, axis=1)
    local = jax.random.randint(jax.random.fold_in(inner, 2), (devices, QD * K), 0, NEG_DEV).astype(jnp.int32)
    ids = inverse[owner_slot * NEG_DEV + local]
    return ids.reshape(QUERIES, K)


def table_rows(key):
    inner = jax.random.fold_in(key, 11)
    return jnp.clip(jax.random.normal(inner, (NEG_DEV * N_DP, D), jnp.float32), -6.0, 6.0)


def mixing():
    near = 102.4 / D
    noise = 0.8 * near
    spread = near * near * K + noise * noise
    pull = 7.5 / (0.0625 * D * spread)
    return (near, noise, pull)


def query_base(key):
    near, noise, pull = mixing()
    table = table_rows(key)
    home = home_rows(key)
    rows = home[id_rows(key)]
    summed = jnp.zeros((QUERIES, D), jnp.float32)
    for slot in range(K):
        summed = summed + table[rows[:, slot]]
    jitter = jnp.clip(jax.random.normal(jax.random.fold_in(key, 19), (QUERIES, D), jnp.float32), -6.0, 6.0)
    return near * summed + noise * jitter


def draw_neg_home(key, part):
    home = home_rows(key)
    return home


def draw_neg_ids(key, part):
    ids = id_rows(key)
    return ids


def draw_neg_table(key, part):
    table = table_rows(key)
    return table.astype(jnp.bfloat16)


def draw_queries(key, part):
    base = query_base(key)
    return jnp.clip(base, -24.0, 24.0).astype(jnp.bfloat16)


def draw_passages(key, part):
    near, noise, pull = mixing()
    base = query_base(key)
    key = jax.random.fold_in(key, 23)
    group_p = PD * N_BLK
    group_q = QD * N_BLK
    index = jnp.arange(PASSAGES, dtype=jnp.int32)
    group = index // group_p
    within = index % group_p
    device = within // PD
    offset = within % PD
    drawn = jax.random.randint(jax.random.fold_in(key, 1), (PASSAGES,), 0, group_q).astype(jnp.int32)
    target = jnp.where(offset < QD, device * QD + offset, drawn).astype(jnp.int32)
    aligned = base[group * group_q + target]
    jitter = jnp.clip(jax.random.normal(jax.random.fold_in(key, 2), (PASSAGES, D), jnp.float32), -6.0, 6.0)
    return jnp.clip(0.3 * jitter + pull * aligned, -6.0, 6.0).astype(jnp.bfloat16)


def plant(values, rng, least, high):
    dims = values.shape
    spot = [jax.random.randint(jax.random.fold_in(rng, axis), (), 0, dims[axis]) for axis in range(len(dims))]
    values = values.at[tuple(spot)].set(least)
    longest = dims.index(max(dims))
    spot[longest] = (spot[longest] + 1) % dims[longest]
    return values.at[tuple(spot)].set(high)


def setup_inputs(seed: int = 0) -> dict:
    key_list = jax.random.split(jax.random.key(seed), 7)
    queries = draw_queries(jax.random.fold_in(key_list[6], 71), 0)
    passages = draw_passages(jax.random.fold_in(key_list[6], 71), 0)
    neg_table = draw_neg_table(jax.random.fold_in(key_list[6], 71), 0)
    neg_ids = draw_neg_ids(jax.random.fold_in(key_list[6], 71), 0)
    counts = plant(jax.random.randint(key_list[4], (QUERIES,), 1, K + 1), jax.random.fold_in(key_list[4], 1), 1, K).astype(jnp.int32)
    neg_home = draw_neg_home(jax.random.fold_in(key_list[6], 71), 0)
    return {"queries": queries, "passages": passages, "neg_table": neg_table, "neg_ids": neg_ids, "counts": counts, "neg_home": neg_home}


score_scale = 0.0625


def reference(queries, passages, neg_table, neg_ids, counts, neg_home):
    group_q = QD * N_BLK
    group_p = PD * N_BLK
    groups = QUERIES // group_q
    query_sets = queries.reshape(groups, group_q, D)
    passage_sets = passages.reshape(groups, group_p, D)
    id_sets = neg_ids.reshape(groups, group_q, K)
    count_sets = counts.reshape(groups, group_q)
    local = jnp.arange(group_q, dtype=jnp.int32)
    pos_col = ((local // QD) * PD + local % QD).astype(jnp.int32)

    def one_group(items):
        query, passage, idx, cnt = items
        scores = score_scale * jnp.dot(query, passage.T, preferred_element_type=jnp.float32)
        negatives = neg_table[neg_home[idx]]
        neg_scores = score_scale * jnp.einsum("qd,qkd->qk", query.astype(jnp.float32), negatives.astype(jnp.float32))
        live = jnp.arange(K, dtype=jnp.int32)[None, :] < cnt[:, None]
        top = jnp.maximum(jnp.max(scores, 1), jnp.max(jnp.where(live, neg_scores, -jnp.inf), 1))
        total = jnp.sum(jnp.exp(scores - top[:, None]), 1) + jnp.sum(jnp.where(live, jnp.exp(neg_scores - top[:, None]), jnp.float32(0.0)), 1)
        lse = top + jnp.log(total)
        positive = passage[pos_col]
        pos_score = score_scale * jnp.sum(query.astype(jnp.float32) * positive.astype(jnp.float32), 1)
        loss = lse - pos_score
        weights = jnp.exp(scores - lse[:, None]).astype(jnp.bfloat16)
        neg_weights = jnp.where(live, jnp.exp(neg_scores - lse[:, None]), jnp.float32(0.0)).astype(jnp.bfloat16)
        grad_q = score_scale * (jnp.dot(weights, passage, preferred_element_type=jnp.float32)
                                + jnp.einsum("qk,qkd->qd", neg_weights.astype(jnp.float32), negatives.astype(jnp.float32))
                                - positive.astype(jnp.float32))
        grad_p = score_scale * jnp.dot(weights.T, query, preferred_element_type=jnp.float32)
        grad_p = grad_p.at[pos_col].add(-score_scale * query.astype(jnp.float32))
        return loss, grad_q.astype(jnp.bfloat16), grad_p.astype(jnp.bfloat16)

    loss, grad_q, grad_p = lax.map(one_group, (query_sets, passage_sets, id_sets, count_sets))
    return loss.reshape(QUERIES), grad_q.reshape(QUERIES, D), grad_p.reshape(PASSAGES, D)
```

```python
import functools

import jax
import jax.numpy as jnp
from jax import lax
from jax.experimental import pallas as pl
from jax.experimental.pallas import tpu as pltpu
from jax.sharding import PartitionSpec as P

MESH = pl.DeviceIdType.MESH
F32, BF16, I32 = jnp.float32, jnp.bfloat16, jnp.int32
SCALE = 0.0625
META = 128
PIECES = 4
SUBS = 2


def nn(a, b):
    return jnp.dot(a, b, preferred_element_type=F32)


def nt(a, b):
    return lax.dot_general(a, b, (((1,), (1,)), ((), ())), preferred_element_type=F32)


def tn(a, b):
    return lax.dot_general(a, b, (((0,), (0,)), ((), ())), preferred_element_type=F32)


def iota(shape, dim):
    return lax.broadcasted_iota(I32, shape, dim)


def to_row(col):
    n = col.shape[0]
    eye = iota((n, n), 0) == iota((n, n), 1)
    return jnp.sum(jnp.where(eye, col, jnp.zeros_like(col)), 0, keepdims=True)


def to_col(row):
    n = row.shape[1]
    eye = iota((n, n), 0) == iota((n, n), 1)
    return jnp.sum(jnp.where(eye, row, jnp.zeros_like(row)), 1, keepdims=True)


def one_hot(cond):
    return jnp.where(cond, 1.0, 0.0).astype(BF16)


def loop(n, body):
    lax.fori_loop(0, n, lambda t, carry: (body(t), carry)[1], 0)


def exchange_kernel(
    n_dp, q_hbm, p_hbm, t_hbm, ids_ref, counts_ref, home_ref,
    qall_hbm, w_ref, gq_ref, loss_ref,
    qv, pv, tv, s_ref, e_ref, mcol, lcol, ob, base, arecv, grecv,
    req_out, req_in, ret_out, ret_in, qr, sneg, eneg, oneg,
    st_out, st_in, lse_out, lse_in,
    local_sem, out_sem, ag_s, ag_r, rs_s, rs_r, st_s, st_r, ls_s, ls_r,
    rq_s, rq_r, rt_s, rt_r,
):
    qd, d = q_hbm.shape
    pd = p_hbm.shape[0]
    half, piece = qd // 2, d // PIECES
    sub = half // SUBS
    slots = ids_ref.shape[1]
    nx = 4
    dp, me = lax.axis_index("dp"), lax.axis_index("blk")
    right = (dp, lax.rem(me + 1, nx))
    left = (dp, lax.rem(me + nx - 1, nx))
    across = (dp, lax.rem(me + 2, nx))

    barrier = pltpu.get_barrier_semaphore()
    for peer in (right, left, across):
        pl.semaphore_signal(barrier, inc=1, device_id=peer, device_id_type=MESH)

    def greet(j):
        peer = lax.rem(dp + j + 1, n_dp)
        pl.semaphore_signal(barrier, inc=1, device_id=(peer, me), device_id_type=MESH)

    loop(n_dp - 1, greet)
    q_in = pltpu.make_async_copy(q_hbm, qv.at[pl.ds(0, qd)], local_sem.at[0])
    p_in = pltpu.make_async_copy(p_hbm, pv, local_sem.at[1])
    t_in = pltpu.make_async_copy(t_hbm, tv, local_sem.at[2])
    q_in.start()
    p_in.start()
    t_in.start()
    pl.semaphore_wait(barrier, n_dp + 2)

    def remote(src, dst, send, recv, peer):
        return pltpu.make_async_remote_copy(
            src_ref=src, dst_ref=dst, send_sem=send, recv_sem=recv, device_id=peer, device_id_type=MESH
        )

    def rows(slot, part):
        return pl.ds(slot * qd + part * half, half)

    def gather_step(i, src, slot, part, peer):
        return remote(src, qv.at[rows(slot, part)], ag_s.at[i], ag_r.at[i], peer)

    own = [q_hbm.at[pl.ds(0, half)], q_hbm.at[pl.ds(half, half)]]
    ag_r1 = gather_step(0, own[0], 1, 0, right)
    ag_l1 = gather_step(1, own[1], 2, 1, left)
    ag_r2 = gather_step(2, own[1], 1, 1, right)
    ag_l2 = gather_step(3, own[0], 2, 0, left)
    ag_r3 = gather_step(4, qv.at[rows(1, 0)], 3, 0, right)
    ag_l3 = gather_step(5, qv.at[rows(2, 1)], 3, 1, left)
    for copy in (ag_r1, ag_l1, ag_r2, ag_l2):
        copy.start()

    n_msg = n_dp * 16
    ids = ids_ref[...]
    home = home_ref[...]
    live = iota((qd, slots), 1) < to_col(counts_ref[...])
    id_hi, id_lo = lax.shift_right_logical(ids, 7), lax.bitwise_and(ids, 127)
    book = jnp.concatenate([lax.shift_right_logical(home, 7), lax.bitwise_and(home, 127)], 1)
    book = book.astype(F32).astype(BF16)
    n_hi = home.shape[0]
    lane = iota((qd, META), 1)
    meta_hi = jnp.zeros((qd, META), F32)
    meta_lo = jnp.zeros((qd, META), F32)
    owner = None
    for k in range(slots):
        pick = one_hot(id_hi[:, k : k + 1] == iota((qd, n_hi), 1))
        found = nn(pick, book)
        found = found[:, :128] * 128.0 + found[:, 128:]
        found = jnp.where(id_lo[:, k : k + 1] == iota((qd, 128), 1), found, 0.0)
        row = jnp.sum(found, 1, keepdims=True).astype(I32)
        if owner is None:
            owner = lax.shift_right_logical(row, 10)
        place = lax.bitwise_and(row, 1023)
        hi = jnp.where(live[:, k : k + 1], lax.shift_right_logical(place, 5), -1).astype(F32)
        lo = lax.bitwise_and(place, 31).astype(F32)
        meta_hi = jnp.where(lane == k, hi, meta_hi)
        meta_lo = jnp.where(lane == k, lo, meta_lo)
    meta_hi, meta_lo = meta_hi.astype(BF16), meta_lo.astype(BF16)

    def message_rows(who, c):
        t, i = iota((n_msg, qd), 0), iota((n_msg, qd), 1)
        return one_hot(
            (lax.shift_right_logical(t, 4) == who)
            & (lax.bitwise_and(lax.shift_right_logical(t, 2), 3) == c)
            & (lax.bitwise_and(t, 3) == lax.bitwise_and(i, 3))
        )

    def query_rows(who, c):
        i, t = iota((qd, n_msg), 0), iota((qd, n_msg), 1)
        return one_hot(
            (lax.shift_right_logical(t, 4) == who)
            & (lax.bitwise_and(lax.shift_right_logical(t, 2), 3) == c)
            & (lax.bitwise_and(t, 3) == lax.bitwise_and(i, 3))
        )

    width = 256

    def fill(buf, mats, src):
        def body(t):
            at = pl.multiple_of(t * width, width)
            total = nn(mats[0], src[pl.ds(0, qd), pl.ds(at, width)])
            for c in range(1, PIECES):
                total += nn(mats[c], src[pl.ds(0, qd), pl.ds(pl.multiple_of(at + c * piece, width), width)])
            buf[:, pl.ds(at, width)] = total.astype(BF16)

        loop(piece // width, body)

    def deliver(out, inn, send, recv):
        def copy(j, frm):
            to = lax.rem(dp + j, n_dp)
            return remote(
                out.at[pl.ds(pl.multiple_of(to * 16, 16), 16)],
                inn.at[pl.ds(pl.multiple_of(frm * 16, 16), 16)],
                send.at[j], recv.at[j], (to, me),
            )

        def came(j):
            return copy(j, lax.rem(dp + n_dp - j, n_dp))

        def begin():
            loop(n_dp - 1, lambda j: copy(j + 1, dp).start())
            mine = pl.ds(pl.multiple_of(dp * 16, 16), 16)
            inn[mine, :] = out[mine, :]

        def arrived():
            loop(n_dp - 1, lambda j: came(j + 1).wait_recv())

        def sent():
            loop(n_dp - 1, lambda j: came(j + 1).wait_send())

        return begin, arrived, sent

    request, request_in, request_sent = deliver(req_out, req_in, rq_s, rq_r)
    answer, answer_in, answer_sent = deliver(ret_out, ret_in, rt_s, rt_r)

    q_in.wait()
    owner_row = to_row(owner)
    pack = [message_rows(owner_row, c) for c in range(PIECES)]
    fill(req_out, pack, qv)
    req_out[:, piece:] = (nn(pack[0], meta_hi) + nn(pack[1], meta_lo)).astype(BF16)
    request()

    def scores(at, n):
        def body(t):
            cols = pl.ds(pl.multiple_of(t * width, width), width)
            s_ref[pl.ds(at, n), cols] = SCALE * nt(qv[pl.ds(at, n), :], pv[cols, :])

        loop(pd // width, body)
        s = s_ref[pl.ds(at, n), :]
        top = jnp.max(s, 1, keepdims=True)
        e = jnp.exp(s - top)
        mcol[pl.ds(at, n), :] = jnp.broadcast_to(top, (n, 128))
        lcol[pl.ds(at, n), :] = jnp.broadcast_to(jnp.sum(e, 1, keepdims=True), (n, 128))
        e_ref[pl.ds(0, n), :] = e.astype(BF16)

    def sums(n, dst, at):
        def body(t):
            cols = pl.ds(pl.multiple_of(t * 512, 512), 512)
            dst[pl.ds(at, n), cols] = nn(e_ref[pl.ds(0, n), :], pv[:, cols]).astype(dst.dtype)

        loop(d // 512, body)

    def chunk(slot, part):
        scores(slot * qd + part * half, half)
        sums(half, ob, (slot - 1) * qd + part * half)

    p_in.wait()
    scores(0, qd)
    sums(qd, base, 0)

    ag_r1.wait_recv()
    ag_r3.start()
    ag_l1.wait_recv()
    ag_l3.start()
    chunk(1, 0)
    chunk(2, 1)

    request_in()
    t_in.wait()
    unpack = [query_rows(lax.shift_right_logical(iota((qd, 1), 0), 2), c) for c in range(PIECES)]

    def unpack_body(t):
        at = pl.multiple_of(t * width, width)
        for c in range(PIECES):
            cols = pl.ds(pl.multiple_of(at + c * piece, width), width)
            qr[:, cols] = nn(unpack[c], req_in[:, pl.ds(at, width)]).astype(BF16)

    loop(piece // width, unpack_body)
    tail = req_in[:, piece:]
    places = nn(unpack[0], tail) * 32.0 + nn(unpack[1], tail)
    mcol[pl.ds(nx * qd, qd), :] = places

    def neg_scores(t):
        cols = pl.ds(pl.multiple_of(t * width, width), width)
        sneg[:, cols] = SCALE * nt(qr[...], tv[cols, :])

    n_rows = tv.shape[0]
    loop(n_rows // width, neg_scores)

    def neg_weights(t):
        at = pl.ds(pl.multiple_of(t * 16, 16), 16)
        where = mcol[pl.ds(pl.multiple_of(nx * qd + t * 16, 16), 16), :]
        s = sneg[at, :]
        col = iota((16, n_rows), 1).astype(F32)
        times = jnp.zeros((16, n_rows), F32)
        for k in range(slots):
            times += jnp.where(where[:, k : k + 1] == col, 1.0, 0.0)
        named = times > 0.0
        top = jnp.max(jnp.where(named, s, -jnp.inf), 1, keepdims=True)
        e = jnp.where(named, times * jnp.exp(jnp.where(named, s - top, 0.0)), 0.0)
        eneg[at, :] = e.astype(BF16)
        sneg[at, pl.ds(0, 128)] = jnp.broadcast_to(top, (16, 128))
        sneg[at, pl.ds(128, 128)] = jnp.broadcast_to(jnp.sum(e, 1, keepdims=True), (16, 128))

    loop(qd // 16, neg_weights)

    def neg_sums(t):
        cols = pl.ds(pl.multiple_of(t * 512, 512), 512)
        oneg[:, cols] = nn(eneg[...], tv[:, cols]).astype(BF16)

    loop(d // 512, neg_sums)
    back = [message_rows(lax.shift_right_logical(iota((1, qd), 1), 2), c) for c in range(PIECES)]
    fill(ret_out, back, oneg)
    rest = jnp.where(lane == 0, sneg[:, :128], jnp.where(lane == 1, sneg[:, 128:256], 0.0))
    tail = jnp.zeros((n_msg, META), F32)
    for c in range(3):
        part = rest.astype(BF16)
        rest = rest - part.astype(F32)
        tail += nn(back[c], part)
    ret_out[:, piece:] = tail.astype(BF16)
    answer()

    ag_r2.wait_recv()
    chunk(1, 1)
    ag_l2.wait_recv()
    chunk(2, 0)

    def back_step(i, src, dst, peer):
        return remote(src, dst, rs_s.at[i], rs_r.at[i], peer)

    def ob_rows(slot, part, k=0, n=half):
        return pl.ds((slot - 1) * qd + part * half + k * sub, n)

    ag_r3.wait_recv()
    b_r = back_step(0, ob.at[ob_rows(2, 1)], grecv.at[0, pl.ds(half, half)], right)
    b_r.start()
    ag_l3.wait_recv()
    b_l = back_step(1, ob.at[ob_rows(1, 0)], grecv.at[1, pl.ds(0, half)], left)
    b_l.start()
    a_r, a_l, c_r, c_l = [], [], [], []
    for k in range(SUBS):
        a_r.append(back_step(2 + 4 * k, ob.at[ob_rows(3, 0, k, sub)], arecv.at[0, pl.ds(k * sub, sub)], right))
        a_l.append(back_step(3 + 4 * k, ob.at[ob_rows(3, 1, k, sub)], arecv.at[1, pl.ds(k * sub, sub)], left))
        c_r.append(back_step(4 + 4 * k, ob.at[ob_rows(2, 0, k, sub)], grecv.at[0, pl.ds(k * sub, sub)], right))
        c_l.append(
            back_step(5 + 4 * k, ob.at[ob_rows(1, 1, k, sub)], grecv.at[1, pl.ds(half + k * sub, sub)], left)
        )
    chunk(3, 0)
    for k in range(SUBS):
        a_r[k].start()
    chunk(3, 1)
    for k in range(SUBS):
        a_l[k].start()

    for entry, slot in enumerate((2, 3, 1, 3)):
        at = pl.ds(slot * qd, qd)
        m_row, l_row = to_row(mcol[at, :1]), to_row(lcol[at, :1])
        st_out[entry, :, :] = jnp.where(iota((8, qd), 0) == 0, m_row, l_row)
    st_right = remote(st_out.at[pl.ds(0, 2)], st_in.at[pl.ds(0, 2)], st_s.at[0], st_r.at[0], right)
    st_left = remote(st_out.at[pl.ds(2, 2)], st_in.at[pl.ds(2, 2)], st_s.at[1], st_r.at[1], left)
    st_across = remote(st_out.at[pl.ds(1, 1)], st_in.at[pl.ds(4, 1)], st_s.at[2], st_r.at[2], across)
    for copy in (st_right, st_left, st_across):
        copy.start()

    answer_in()
    opened = [query_rows(owner, c) for c in range(PIECES)]
    tail = ret_in[:, piece:]
    neg_stats = nn(opened[0], tail) + nn(opened[1], tail) + nn(opened[2], tail)
    for copy in (st_right, st_left, st_across):
        copy.wait_recv()

    def stat(entry, i):
        return to_col(st_in[entry, i : i + 1, :])

    m_own, l_own = mcol[pl.ds(0, qd), :1], lcol[pl.ds(0, qd), :1]
    m_l, l_l, m_r, l_r, m_x, l_x = (stat(e, i) for e in (0, 2, 4) for i in (0, 1))
    m_n, l_n = neg_stats[:, 0:1], neg_stats[:, 1:2]
    pairs = ((m_own, l_own), (m_l, l_l), (m_r, l_r), (m_x, l_x), (m_n, l_n))
    top = functools.reduce(jnp.maximum, [m for m, _ in pairs])
    lse = top + jnp.log(sum(l * jnp.exp(m - top) for m, l in pairs))
    lse_row = to_row(lse)
    lse_out[...] = jnp.broadcast_to(lse_row, (8, qd))
    lse_copies = [
        remote(lse_out, lse_in.at[i], ls_s.at[i], ls_r.at[i], peer)
        for i, peer in enumerate((right, left, across))
    ]
    for copy in lse_copies:
        copy.start()
    eye = iota((qd, qd), 0) == iota((qd, qd), 1)
    positive = jnp.sum(jnp.where(eye, s_ref[pl.ds(0, qd), pl.ds(0, qd)], 0.0), 0, keepdims=True)
    loss_ref[...] = lse_row - positive

    f_own, f_n = jnp.exp(m_own - lse), jnp.exp(m_n - lse)

    def base_body(t):
        at = pl.multiple_of(t * width, width)
        for c in range(PIECES):
            cols = pl.ds(pl.multiple_of(at + c * piece, width), width)
            neg = nn(opened[c], ret_in[:, pl.ds(at, width)])
            base[:, cols] = f_own * base[:, cols] + f_n * neg - pv[pl.ds(0, qd), cols].astype(F32)

    loop(piece // width, base_body)

    w_ref[pl.ds(0, qd), :] = jnp.exp(s_ref[pl.ds(0, qd), :] - lse).astype(BF16)
    for i in range(3):
        lse_copies[i].wait_recv()
        at = pl.ds((i + 1) * qd, qd)
        w_ref[at, :] = jnp.exp(s_ref[at, :] - to_col(lse_in[i, 0:1, :])).astype(BF16)
    spill = pltpu.make_async_copy(qv, qall_hbm, out_sem.at[0])
    spill.start()

    def merge(slot, part, m_far, src):
        m_near = mcol[pl.ds(slot * qd + part * half, half), :1]
        m_far = m_far[part * half : (part + 1) * half]
        both = jnp.maximum(m_near, m_far)
        f_near, f_far = jnp.exp(m_near - both), jnp.exp(m_far - both)

        def add(k):
            at = ob_rows(slot, part, k, sub)
            near, far = f_near[k * sub : (k + 1) * sub], f_far[k * sub : (k + 1) * sub]

            def body(t):
                cols = pl.ds(pl.multiple_of(t * 512, 512), 512)
                total = near * ob[at, cols].astype(F32) + far * src[pl.ds(k * sub, sub), cols].astype(F32)
                ob[at, cols] = total.astype(BF16)

            loop(d // 512, body)

        return add

    merge_r = merge(2, 0, stat(1, 0), arecv.at[0])
    merge_l = merge(1, 1, stat(3, 0), arecv.at[1])
    for k in range(SUBS):
        a_r[k].wait_recv()
        merge_r(k)
        c_r[k].start()
        a_l[k].wait_recv()
        merge_l(k)
        c_l[k].start()

    top_l, top_r = jnp.maximum(m_l, m_x), jnp.maximum(m_r, m_x)
    first = iota((qd, 1), 0) < half
    f_l = jnp.exp(jnp.where(first, top_l, m_l) - lse)
    f_r = jnp.exp(jnp.where(first, m_r, top_r) - lse)

    def finish(at, n):
        near_l, near_r = f_l[at : at + n], f_r[at : at + n]

        def body(t):
            cols = pl.ds(pl.multiple_of(t * 512, 512), 512)
            total = base[pl.ds(at, n), cols]
            total += near_l * grecv[0, pl.ds(at, n), cols].astype(F32)
            total += near_r * grecv[1, pl.ds(at, n), cols].astype(F32)
            gq_ref[pl.ds(at, n), cols] = (SCALE * total).astype(BF16)

        loop(d // 512, body)

    b_r.wait_recv()
    b_l.wait_recv()
    for k in range(SUBS):
        c_r[k].wait_recv()
        finish(k * sub, sub)
        c_l[k].wait_recv()
        finish(half + k * sub, sub)

    spill.wait()
    for copy in (ag_r1, ag_r2, ag_r3, ag_l1, ag_l2, ag_l3, b_r, b_l, *a_r, *a_l, *c_r, *c_l):
        copy.wait_send()
    for copy in (st_right, st_left, st_across, *lse_copies):
        copy.wait_send()
    request_sent()
    answer_sent()


def passage_kernel(w_ref, q_ref, gq_in, gp_ref, gq_ref):
    qd = gq_in.shape[0]
    total = tn(w_ref[...], q_ref[...])
    gp_ref[...] = (SCALE * total).astype(BF16)
    gp_ref[pl.ds(0, qd), :] = (SCALE * (total[:qd] - q_ref[pl.ds(0, qd), :].astype(F32))).astype(BF16)
    gq_ref[...] = gq_in[...]


def per_device(n_dp, queries, passages, neg_table, neg_ids, counts, neg_home):
    qd, d = queries.shape
    pd = passages.shape[0]
    n_rows = neg_table.shape[0]
    nx, half = 4, qd // 2
    n_msg, piece = n_dp * 16, d // PIECES
    any_spec = pl.BlockSpec(memory_space=pl.ANY)
    vmem_spec = pl.BlockSpec(memory_space=pltpu.VMEM)
    dma = pltpu.SemaphoreType.DMA
    qall, w, gq, loss = pl.pallas_call(
        functools.partial(exchange_kernel, n_dp),
        out_shape=(
            jax.ShapeDtypeStruct((nx * qd, d), BF16),
            jax.ShapeDtypeStruct((nx * qd, pd), BF16),
            jax.ShapeDtypeStruct((qd, d), BF16),
            jax.ShapeDtypeStruct((1, qd), F32),
        ),
        in_specs=[any_spec] * 3 + [vmem_spec] * 3,
        out_specs=(any_spec, vmem_spec, vmem_spec, vmem_spec),
        scratch_shapes=[
            pltpu.VMEM((nx * qd, d), BF16),
            pltpu.VMEM((pd, d), BF16),
            pltpu.VMEM((n_rows, d), BF16),
            pltpu.VMEM((nx * qd, pd), F32),
            pltpu.VMEM((qd, pd), BF16),
            pltpu.VMEM(((nx + 1) * qd, 128), F32),
            pltpu.VMEM((nx * qd, 128), F32),
            pltpu.VMEM(((nx - 1) * qd, d), BF16),
            pltpu.VMEM((qd, d), F32),
            pltpu.VMEM((2, half, d), BF16),
            pltpu.VMEM((2, qd, d), BF16),
            pltpu.VMEM((n_msg, piece + META), BF16),
            pltpu.VMEM((n_msg, piece + META), BF16),
            pltpu.VMEM((n_msg, piece + META), BF16),
            pltpu.VMEM((n_msg, piece + META), BF16),
            pltpu.VMEM((qd, d), BF16),
            pltpu.VMEM((qd, n_rows), F32),
            pltpu.VMEM((qd, n_rows), BF16),
            pltpu.VMEM((qd, d), BF16),
            pltpu.VMEM((4, 8, qd), F32),
            pltpu.VMEM((5, 8, qd), F32),
            pltpu.VMEM((8, qd), F32),
            pltpu.VMEM((3, 8, qd), F32),
            dma((3,)),
            dma((1,)),
            dma((6,)),
            dma((6,)),
            dma((2 + 4 * SUBS,)),
            dma((2 + 4 * SUBS,)),
            dma((3,)),
            dma((3,)),
            dma((3,)),
            dma((3,)),
            dma((n_dp,)),
            dma((n_dp,)),
            dma((n_dp,)),
            dma((n_dp,)),
        ],
        compiler_params=pltpu.CompilerParams(
            collective_id=0, has_side_effects=True, vmem_limit_bytes=56 * 1024 * 1024
        ),
        cost_estimate=pl.CostEstimate(flops=9_000_000_000, bytes_accessed=25_000_000, transcendentals=1_000_000),
        name="exchange",
    )(queries, passages, neg_table, neg_ids, counts.reshape(1, qd), neg_home.reshape(-1, 128))
    tile = 512
    grad_p, grad_q = pl.pallas_call(
        passage_kernel,
        grid=(d // tile,),
        out_shape=(jax.ShapeDtypeStruct((pd, d), BF16), jax.ShapeDtypeStruct((qd, d), BF16)),
        in_specs=[
            pl.BlockSpec((nx * qd, pd), lambda t: (0, 0)),
            pl.BlockSpec((nx * qd, tile), lambda t: (0, t)),
            pl.BlockSpec((qd, tile), lambda t: (0, t)),
        ],
        out_specs=(
            pl.BlockSpec((pd, tile), lambda t: (0, t)),
            pl.BlockSpec((qd, tile), lambda t: (0, t)),
        ),
        compiler_params=pltpu.CompilerParams(vmem_limit_bytes=32 * 1024 * 1024),
        cost_estimate=pl.CostEstimate(flops=3_300_000_000, bytes_accessed=14_000_000, transcendentals=0),
        name="passage_grads",
    )(w, qall, gq)
    return loss.reshape(qd), grad_q, grad_p


def solution(mesh):
    in_specs = (
        P(("dp", "blk"), None),
        P(("dp", "blk"), None),
        P("dp", None),
        P(("dp", "blk"), None),
        P(("dp", "blk")),
        P(),
    )
    out_specs = (P(("dp", "blk")), P(("dp", "blk"), None), P(("dp", "blk"), None))
    return jax.shard_map(
        functools.partial(per_device, mesh.shape["dp"]),
        mesh=mesh, in_specs=in_specs, out_specs=out_specs, check_vma=False,
    )
```

```python
import functools

import jax
import jax.numpy as jnp
from jax import lax
from jax.experimental import pallas as pl
from jax.experimental.pallas import tpu as pltpu
from jax.sharding import PartitionSpec as P

MESH = pl.DeviceIdType.MESH
F32, BF16, I32 = jnp.float32, jnp.bfloat16, jnp.int32
SCALE = 0.0625
META = 128
PIECES = 4
SUBS = 4


def nn(a, b):
    return jnp.dot(a, b, preferred_element_type=F32)


def nt(a, b):
    return lax.dot_general(a, b, (((1,), (1,)), ((), ())), preferred_element_type=F32)


def tn(a, b):
    return lax.dot_general(a, b, (((0,), (0,)), ((), ())), preferred_element_type=F32)


def iota(shape, dim):
    return lax.broadcasted_iota(I32, shape, dim)


def to_row(col):
    n = col.shape[0]
    eye = iota((n, n), 0) == iota((n, n), 1)
    return jnp.sum(jnp.where(eye, col, jnp.zeros_like(col)), 0, keepdims=True)


def to_col(row):
    n = row.shape[1]
    eye = iota((n, n), 0) == iota((n, n), 1)
    return jnp.sum(jnp.where(eye, row, jnp.zeros_like(row)), 1, keepdims=True)


def one_hot(cond):
    return jnp.where(cond, 1.0, 0.0).astype(BF16)


def loop(n, body):
    lax.fori_loop(0, n, lambda t, carry: (body(t), carry)[1], 0)


def message_rows(n_msg, who, c):
    t, i = iota((n_msg, who.shape[1]), 0), iota((n_msg, who.shape[1]), 1)
    return one_hot(
        (lax.shift_right_logical(t, 4) == who)
        & (lax.bitwise_and(lax.shift_right_logical(t, 2), 3) == c)
        & (lax.bitwise_and(t, 3) == lax.bitwise_and(i, 3))
    )


def query_rows(n_msg, who, c):
    i, t = iota((who.shape[0], n_msg), 0), iota((who.shape[0], n_msg), 1)
    return one_hot(
        (lax.shift_right_logical(t, 4) == who)
        & (lax.bitwise_and(lax.shift_right_logical(t, 2), 3) == c)
        & (lax.bitwise_and(t, 3) == lax.bitwise_and(i, 3))
    )


def exchange_kernel(
    n_dp, q_hbm, p_hbm, t_hbm, ids_ref, counts_ref, home_ref,
    gp_ref, gq_ref, loss_ref,
    qv, pv, tv, s_ref, e_ref, wt_ref, stats, ob, base, arecv, grecv,
    req_out, req_in, ret_out, ret_in, qr, sneg, times_ref, eneg, oneg, factors,
    st_out, st_in, lse_out, lse_in,
    local_sem, ag_s, ag_r, rs_s, rs_r, st_s, st_r, ls_s, ls_r,
    rq_s, rq_r, rt_s, rt_r,
):
    qd, d = q_hbm.shape
    pd = p_hbm.shape[0]
    half, piece = qd // 2, d // PIECES
    sub = half // SUBS
    slots = ids_ref.shape[0]
    n_msg = n_dp * 16
    nx = 4
    dp, me = lax.axis_index("dp"), lax.axis_index("blk")
    right = (dp, lax.rem(me + 1, nx))
    left = (dp, lax.rem(me + nx - 1, nx))
    across = (dp, lax.rem(me + 2, nx))

    barrier = pltpu.get_barrier_semaphore()
    for peer in (right, left, across):
        pl.semaphore_signal(barrier, inc=1, device_id=peer, device_id_type=MESH)

    def greet(j):
        peer = lax.rem(dp + j + 1, n_dp)
        pl.semaphore_signal(barrier, inc=1, device_id=(peer, me), device_id_type=MESH)

    loop(n_dp - 1, greet)
    q_in = pltpu.make_async_copy(q_hbm, qv.at[pl.ds(0, qd)], local_sem.at[0])
    p_in = pltpu.make_async_copy(p_hbm, pv, local_sem.at[1])
    t_in = pltpu.make_async_copy(t_hbm, tv, local_sem.at[2])
    q_in.start()
    p_in.start()
    t_in.start()
    pl.semaphore_wait(barrier, n_dp + 2)

    def remote(src, dst, send, recv, peer):
        return pltpu.make_async_remote_copy(
            src_ref=src, dst_ref=dst, send_sem=send, recv_sem=recv, device_id=peer, device_id_type=MESH
        )

    def half_rows(block, part, k=0, n=half):
        return pl.ds(block * qd + part * half + k * sub, n)

    def gather_step(i, src, block, part, peer):
        return remote(src, qv.at[half_rows(block, part)], ag_s.at[i], ag_r.at[i], peer)

    own = [q_hbm.at[pl.ds(0, half)], q_hbm.at[pl.ds(half, half)]]
    ag_r1 = gather_step(0, own[0], 1, 0, right)
    ag_l1 = gather_step(1, own[1], 1, 1, left)
    ag_r2 = gather_step(2, own[1], 2, 1, right)
    ag_l2 = gather_step(3, own[0], 2, 0, left)
    ag_r3 = gather_step(4, qv.at[half_rows(1, 0)], 3, 0, right)
    ag_l3 = gather_step(5, qv.at[half_rows(1, 1)], 3, 1, left)
    for copy in (ag_r1, ag_l1, ag_r2, ag_l2):
        copy.start()

    ids, home = ids_ref[...], home_ref[...]
    book = jnp.concatenate([lax.shift_right_logical(home, 7), lax.bitwise_and(home, 127)], 1)
    book = book.astype(F32).T.astype(BF16)
    n_hi = home.shape[0]
    together = 4
    named_rows = []
    for k in range(0, slots, together):
        id_row = jnp.concatenate([ids[k + i : k + i + 1] for i in range(together)], 1)
        pick = one_hot(lax.shift_right_logical(id_row, 7) == iota((n_hi, together * qd), 0))
        found = nn(book, pick)
        found = found[:128] * 128.0 + found[128:]
        mine = lax.bitwise_and(id_row, 127) == iota((128, together * qd), 0)
        row = jnp.sum(jnp.where(mine, found, 0.0), 0, keepdims=True).astype(I32)
        named_rows += [row[:, i * qd : (i + 1) * qd] for i in range(together)]
    rows = jnp.zeros((slots, qd), I32)
    for k in range(slots):
        rows = jnp.where(iota((slots, qd), 0) == k, named_rows[k], rows)
    live = iota((slots, qd), 0) < counts_ref[...]
    place = lax.bitwise_and(rows, 1023)
    meta_hi = jnp.where(live, lax.shift_right_logical(place, 5), -1).astype(F32)
    meta_lo = lax.bitwise_and(place, 31).astype(F32)
    blank = jnp.zeros((META - slots, qd), F32)
    meta_hi = jnp.concatenate([meta_hi, blank], 0).astype(BF16)
    meta_lo = jnp.concatenate([meta_lo, blank], 0).astype(BF16)
    owner_row = lax.shift_right_logical(named_rows[0], 10)
    width = 512

    def fill(buf, mats, src):
        def body(t):
            at = pl.multiple_of(t * width, width)
            total = nn(mats[0], src[pl.ds(0, qd), pl.ds(at, width)])
            for c in range(1, PIECES):
                total += nn(mats[c], src[pl.ds(0, qd), pl.ds(pl.multiple_of(at + c * piece, width), width)])
            buf[:, pl.ds(at, width)] = total.astype(BF16)

        loop(piece // width, body)

    def deliver(out, inn, send, recv):
        def copy(j, frm):
            to = lax.rem(dp + j, n_dp)
            return remote(
                out.at[pl.ds(pl.multiple_of(to * 16, 16), 16)],
                inn.at[pl.ds(pl.multiple_of(frm * 16, 16), 16)],
                send.at[j], recv.at[j], (to, me),
            )

        def came(j):
            return copy(j, lax.rem(dp + n_dp - j, n_dp))

        def begin():
            loop(n_dp - 1, lambda j: copy(j + 1, dp).start())
            mine = pl.ds(pl.multiple_of(dp * 16, 16), 16)
            inn[mine, :] = out[mine, :]

        def arrived():
            loop(n_dp - 1, lambda j: came(j + 1).wait_recv())

        def sent():
            loop(n_dp - 1, lambda j: came(j + 1).wait_send())

        return begin, arrived, sent

    request, request_in, request_sent = deliver(req_out, req_in, rq_s, rq_r)
    answer, answer_in, answer_sent = deliver(ret_out, ret_in, rt_s, rt_r)

    q_in.wait()
    pack = [message_rows(n_msg, owner_row, c) for c in range(PIECES)]
    fill(req_out, pack, qv)
    req_out[:, piece:] = (nt(pack[0], meta_hi) + nt(pack[1], meta_lo)).astype(BF16)
    request()

    def scores(block):
        cols = pl.ds(block * qd, qd)
        s_ref[:, cols] = SCALE * nt(pv[...], qv[cols, :])
        s = s_ref[:, cols]
        top = jnp.max(s, 0, keepdims=True)
        e = jnp.exp(s - top)
        stats[block, 0:1, :] = top
        stats[block, 1:2, :] = jnp.sum(e, 0, keepdims=True)
        for j in range(pd // 128):
            e_ref[:, j * 128 : (j + 1) * 128] = e[j * 128 : (j + 1) * 128].T.astype(BF16)

    wide = 2048

    def sums(dst, at):
        def body(t):
            cols = pl.ds(pl.multiple_of(t * wide, wide), wide)
            dst[pl.ds(at, qd), cols] = nn(e_ref[...], pv[:, cols]).astype(dst.dtype)

        loop(d // wide, body)

    p_in.wait()
    scores(0)
    sums(base, 0)

    ag_r1.wait_recv()
    ag_r3.start()
    ag_l1.wait_recv()
    ag_l3.start()
    scores(1)
    sums(ob, 0)

    request_in()
    t_in.wait()
    asker = lax.shift_right_logical(iota((qd, 1), 0), 2)
    for c in range(PIECES):
        qr[:, c * piece : (c + 1) * piece] = nn(query_rows(n_msg, asker, c), req_in[:, :piece]).astype(BF16)
    asker = lax.shift_right_logical(iota((1, qd), 1), 2)
    back = [message_rows(n_msg, asker, c) for c in range(PIECES)]
    tail = req_in[:, piece:]
    places = tn(tail, back[0]) * 32.0 + tn(tail, back[1])
    sneg[...] = SCALE * nt(tv[...], qr[...])
    n_rows = tv.shape[0]

    def neg_top(t, top):
        at = pl.ds(pl.multiple_of(t * 128, 128), 128)
        index = (iota((128, qd), 0) + t * 128).astype(F32)
        times = jnp.zeros((128, qd), F32)
        for k in range(slots):
            times += jnp.where(places[k : k + 1] == index, 1.0, 0.0)
        times_ref[at, :] = times
        return jnp.maximum(top, jnp.max(jnp.where(times > 0.0, sneg[at, :], -jnp.inf), 0, keepdims=True))

    m_far = lax.fori_loop(0, n_rows // 128, neg_top, jnp.full((1, qd), -jnp.inf, F32))

    def neg_weights(t, total):
        at = pl.ds(pl.multiple_of(t * 128, 128), 128)
        times = times_ref[at, :]
        e = jnp.where(times > 0.0, times * jnp.exp(jnp.minimum(sneg[at, :] - m_far, 0.0)), 0.0)
        eneg[:, at] = e.T.astype(BF16)
        return total + jnp.sum(e, 0, keepdims=True)

    l_far = lax.fori_loop(0, n_rows // 128, neg_weights, jnp.zeros((1, qd), F32))

    def neg_sums(t):
        cols = pl.ds(pl.multiple_of(t * wide, wide), wide)
        oneg[:, cols] = nn(eneg[...], tv[:, cols]).astype(BF16)

    loop(d // wide, neg_sums)
    fill(ret_out, back, oneg)
    line = iota((META, qd), 0)
    rest = jnp.where(line == 0, m_far, jnp.where(line == 1, l_far, 0.0))
    tail = jnp.zeros((n_msg, META), F32)
    for c in range(3):
        part = rest.astype(BF16)
        rest = rest - part.astype(F32)
        tail += nt(back[c], part)
    ret_out[:, piece:] = tail.astype(BF16)
    answer()

    ag_r2.wait_recv()
    ag_l2.wait_recv()
    scores(2)
    sums(ob, qd)

    def back_step(i, block, part, k, n, dst, at, peer):
        src = ob.at[half_rows(block - 1, part, k, n)]
        return remote(src, dst.at[pl.ds(at, n)], rs_s.at[i], rs_r.at[i], peer)

    both, quarter = 2, half // 2
    b_r = [back_step(k, 1, 1, k * SUBS // 2, quarter, grecv.at[0], half + k * quarter, right) for k in range(both)]
    b_l = [back_step(2 + k, 1, 0, k * SUBS // 2, quarter, grecv.at[1], k * quarter, left) for k in range(both)]
    a_r = [back_step(4 + 4 * k, 3, 0, k, sub, arecv.at[0], k * sub, right) for k in range(SUBS)]
    a_l = [back_step(5 + 4 * k, 3, 1, k, sub, arecv.at[1], k * sub, left) for k in range(SUBS)]
    c_r = [back_step(6 + 4 * k, 2, 0, k, sub, grecv.at[0], k * sub, right) for k in range(SUBS)]
    c_l = [back_step(7 + 4 * k, 2, 1, k, sub, grecv.at[1], half + k * sub, left) for k in range(SUBS)]
    b_r[0].start()
    b_l[0].start()
    ag_r3.wait_recv()
    ag_l3.wait_recv()
    scores(3)

    first = iota((8, qd), 1) < half
    picks = [stats[block, :, :] for block in range(nx)]
    st_out[0, :, :] = jnp.where(first, picks[2], picks[1])
    st_out[1, :, :] = picks[3]
    st_out[2, :, :] = jnp.where(first, picks[1], picks[2])
    st_out[3, :, :] = picks[3]
    st_right = remote(st_out.at[pl.ds(0, 2)], st_in.at[pl.ds(0, 2)], st_s.at[0], st_r.at[0], right)
    st_left = remote(st_out.at[pl.ds(2, 2)], st_in.at[pl.ds(2, 2)], st_s.at[1], st_r.at[1], left)
    st_across = remote(st_out.at[pl.ds(1, 1)], st_in.at[pl.ds(4, 1)], st_s.at[2], st_r.at[2], across)
    st_copies = [st_right, st_left, st_across]
    for copy in st_copies:
        copy.start()
    sums(ob, 2 * qd)
    for k in range(SUBS):
        a_r[k].start()
        a_l[k].start()

    answer_in()
    tail = ret_in[:, piece:]
    neg_stats = tn(tail, pack[0]) + tn(tail, pack[1]) + tn(tail, pack[2])
    for copy in st_copies:
        copy.wait_recv()

    def stat(entry, i):
        return st_in[entry, i : i + 1, :]

    m_own, l_own = stats[0, 0:1, :], stats[0, 1:2, :]
    m_l, l_l, m_r, l_r, m_x, l_x = (stat(e, i) for e in (0, 2, 4) for i in (0, 1))
    m_n, l_n = neg_stats[0:1], neg_stats[1:2]
    pairs = ((m_own, l_own), (m_l, l_l), (m_r, l_r), (m_x, l_x), (m_n, l_n))
    top = functools.reduce(jnp.maximum, [m for m, _ in pairs])
    lse = top + jnp.log(sum(l * jnp.exp(m - top) for m, l in pairs))
    lse_out[...] = jnp.broadcast_to(lse, (8, qd))
    lse_copies = [
        remote(lse_out, lse_in.at[i], ls_s.at[i], ls_r.at[i], peer)
        for i, peer in enumerate((right, left, across))
    ]
    for copy in lse_copies:
        copy.start()
    eye = iota((qd, qd), 0) == iota((qd, qd), 1)
    loss_ref[...] = lse - jnp.sum(jnp.where(eye, s_ref[pl.ds(0, qd), pl.ds(0, qd)], 0.0), 0, keepdims=True)

    f_own, f_n = to_col(jnp.exp(m_own - lse)), to_col(jnp.exp(m_n - lse))
    owner_col = to_col(owner_row)
    for c in range(PIECES):
        cols = pl.ds(c * piece, piece)
        neg = nn(query_rows(n_msg, owner_col, c), ret_in[:, :piece])
        base[:, cols] = f_own * base[:, cols] + f_n * neg - pv[pl.ds(0, qd), cols].astype(F32)

    for copy in lse_copies:
        copy.wait_recv()
    front = iota((1, qd), 1) < half
    lse_l, lse_r, lse_x = (lse_in[i, 0:1, :] for i in range(3))
    by_block = (lse, jnp.where(front, lse_l, lse_r), jnp.where(front, lse_r, lse_l), lse_x)
    for block in range(nx):
        cols = pl.ds(block * qd, qd)
        wt_ref[:, cols] = jnp.exp(s_ref[:, cols] - by_block[block]).astype(BF16)
    span = 1024

    def passage_grads(t):
        cols = pl.ds(pl.multiple_of(t * span, span), span)
        total = nn(wt_ref[...], qv[:, cols])
        gp_ref[pl.ds(qd, pd - qd), cols] = (SCALE * total[qd:]).astype(BF16)
        gp_ref[pl.ds(0, qd), cols] = (SCALE * (total[:qd] - qv[pl.ds(0, qd), cols].astype(F32))).astype(BF16)

    loop(d // span, passage_grads)

    m_near = stats[2, 0:1, :]
    m_away = jnp.where(front, stat(1, 0), stat(3, 0))
    m_both = jnp.maximum(m_near, m_away)
    factors[0, :, :] = jnp.broadcast_to(to_col(jnp.exp(m_near - m_both)), (qd, 128))
    factors[1, :, :] = jnp.broadcast_to(to_col(jnp.exp(m_away - m_both)), (qd, 128))

    def merge(part, k):
        at, far_at = part * half + k * sub, pl.ds(k * sub, sub)
        f_near, f_away = factors[0, pl.ds(at, sub), :1], factors[1, pl.ds(at, sub), :1]

        def body(t):
            cols = pl.ds(pl.multiple_of(t * 1024, 1024), 1024)
            here = ob[pl.ds(qd + at, sub), cols].astype(F32)
            total = f_near * here + f_away * arecv[part, far_at, cols].astype(F32)
            ob[pl.ds(qd + at, sub), cols] = total.astype(BF16)

        loop(d // 1024, body)

    for k in range(SUBS):
        a_r[k].wait_send()
        a_l[k].wait_send()
    b_r[1].start()
    b_l[1].start()
    for k in range(SUBS):
        a_r[k].wait_recv()
        merge(0, k)
        c_r[k].start()
        a_l[k].wait_recv()
        merge(1, k)
        c_l[k].start()

    top_l, top_r = jnp.maximum(m_l, m_x), jnp.maximum(m_r, m_x)
    factors[2, :, :] = jnp.broadcast_to(to_col(jnp.exp(jnp.where(front, top_l, m_l) - lse)), (qd, 128))
    factors[3, :, :] = jnp.broadcast_to(to_col(jnp.exp(jnp.where(front, m_r, top_r) - lse)), (qd, 128))

    def finish(at):
        f_l, f_r = factors[2, pl.ds(at, sub), :1], factors[3, pl.ds(at, sub), :1]

        def body(t):
            cols = pl.ds(pl.multiple_of(t * 1024, 1024), 1024)
            total = base[pl.ds(at, sub), cols]
            total += f_l * grecv[0, pl.ds(at, sub), cols].astype(F32)
            total += f_r * grecv[1, pl.ds(at, sub), cols].astype(F32)
            gq_ref[pl.ds(at, sub), cols] = (SCALE * total).astype(BF16)

        loop(d // 1024, body)

    for copy in b_r + b_l:
        copy.wait_recv()
    for k in range(SUBS):
        c_r[k].wait_recv()
        finish(k * sub)
        c_l[k].wait_recv()
        finish(half + k * sub)

    for copy in [ag_r1, ag_r2, ag_r3, ag_l1, ag_l2, ag_l3] + b_r + b_l + c_r + c_l + st_copies + lse_copies:
        copy.wait_send()
    request_sent()
    answer_sent()


def write_kernel(gp_in, gq_in, loss_in, gp_out, gq_out, loss_out, sems):
    parts = 4
    n = gp_in.shape[0] // parts
    copies = [
        pltpu.make_async_copy(gp_in.at[pl.ds(i * n, n)], gp_out.at[pl.ds(i * n, n)], sems.at[i]) for i in range(parts)
    ]
    copies.append(pltpu.make_async_copy(gq_in, gq_out, sems.at[parts]))
    copies.append(pltpu.make_async_copy(loss_in, loss_out, sems.at[parts + 1]))
    for copy in copies:
        copy.start()
    for copy in copies:
        copy.wait()


def per_device(n_dp, queries, passages, neg_table, neg_ids, counts, neg_home):
    qd, d = queries.shape
    pd = passages.shape[0]
    n_rows = neg_table.shape[0]
    nx, half = 4, qd // 2
    n_msg, piece = n_dp * 16, d // PIECES
    any_spec = pl.BlockSpec(memory_space=pl.ANY)
    vmem_spec = pl.BlockSpec(memory_space=pltpu.VMEM)
    dma = pltpu.SemaphoreType.DMA
    grad_p, grad_q, loss = pl.pallas_call(
        functools.partial(exchange_kernel, n_dp),
        out_shape=(
            pltpu.VMEM((pd, d), BF16),
            pltpu.VMEM((qd, d), BF16),
            pltpu.VMEM((1, qd), F32),
        ),
        in_specs=[any_spec] * 3 + [vmem_spec] * 3,
        out_specs=(vmem_spec, vmem_spec, vmem_spec),
        scratch_shapes=[
            pltpu.VMEM((nx * qd, d), BF16),
            pltpu.VMEM((pd, d), BF16),
            pltpu.VMEM((n_rows, d), BF16),
            pltpu.VMEM((pd, nx * qd), F32),
            pltpu.VMEM((qd, pd), BF16),
            pltpu.VMEM((pd, nx * qd), BF16),
            pltpu.VMEM((nx, 8, qd), F32),
            pltpu.VMEM(((nx - 1) * qd, d), BF16),
            pltpu.VMEM((qd, d), F32),
            pltpu.VMEM((2, half, d), BF16),
            pltpu.VMEM((2, qd, d), BF16),
            pltpu.VMEM((n_msg, piece + META), BF16),
            pltpu.VMEM((n_msg, piece + META), BF16),
            pltpu.VMEM((n_msg, piece + META), BF16),
            pltpu.VMEM((n_msg, piece + META), BF16),
            pltpu.VMEM((qd, d), BF16),
            pltpu.VMEM((n_rows, qd), F32),
            pltpu.VMEM((n_rows, qd), F32),
            pltpu.VMEM((qd, n_rows), BF16),
            pltpu.VMEM((qd, d), BF16),
            pltpu.VMEM((4, qd, 128), F32),
            pltpu.VMEM((4, 8, qd), F32),
            pltpu.VMEM((5, 8, qd), F32),
            pltpu.VMEM((8, qd), F32),
            pltpu.VMEM((3, 8, qd), F32),
            dma((3,)),
            dma((6,)),
            dma((6,)),
            dma((4 + 4 * SUBS,)),
            dma((4 + 4 * SUBS,)),
            dma((3,)),
            dma((3,)),
            dma((3,)),
            dma((3,)),
            dma((n_dp,)),
            dma((n_dp,)),
            dma((n_dp,)),
            dma((n_dp,)),
        ],
        compiler_params=pltpu.CompilerParams(
            collective_id=0, has_side_effects=True, vmem_limit_bytes=54 * 1024 * 1024
        ),
        cost_estimate=pl.CostEstimate(flops=13_000_000_000, bytes_accessed=25_000_000, transcendentals=1_000_000),
        name="exchange",
    )(queries, passages, neg_table, neg_ids.T, counts.reshape(1, qd), neg_home.reshape(-1, 128))
    grad_p, grad_q, loss = pl.pallas_call(
        write_kernel,
        out_shape=(
            jax.ShapeDtypeStruct((pd, d), BF16),
            jax.ShapeDtypeStruct((qd, d), BF16),
            jax.ShapeDtypeStruct((1, qd), F32),
        ),
        in_specs=[any_spec] * 3,
        out_specs=(any_spec, any_spec, any_spec),
        scratch_shapes=[dma((6,))],
        compiler_params=pltpu.CompilerParams(vmem_limit_bytes=1024 * 1024),
        cost_estimate=pl.CostEstimate(flops=0, bytes_accessed=7_300_000, transcendentals=0),
        name="write",
    )(grad_p, grad_q, loss)
    return loss.reshape(qd), grad_q, grad_p


def solution(mesh):
    in_specs = (
        P(("dp", "blk"), None),
        P(("dp", "blk"), None),
        P("dp", None),
        P(("dp", "blk"), None),
        P(("dp", "blk")),
        P(),
    )
    out_specs = (P(("dp", "blk")), P(("dp", "blk"), None), P(("dp", "blk"), None))
    return jax.shard_map(
        functools.partial(per_device, mesh.shape["dp"]),
        mesh=mesh, in_specs=in_specs, out_specs=out_specs, check_vma=False,
    )
```

```python
import functools

import jax
import jax.numpy as jnp
from jax import lax
from jax.experimental import pallas as pl
from jax.experimental.pallas import tpu as pltpu
from jax.sharding import PartitionSpec as P

MESH = pl.DeviceIdType.MESH
F32, BF16, I32 = jnp.float32, jnp.bfloat16, jnp.int32
SCALE = 0.0625
META = 128
PIECES = 4
SUBS = 4


def nn(a, b):
    return jnp.dot(a, b, preferred_element_type=F32)


def nt(a, b):
    return lax.dot_general(a, b, (((1,), (1,)), ((), ())), preferred_element_type=F32)


def tn(a, b):
    return lax.dot_general(a, b, (((0,), (0,)), ((), ())), preferred_element_type=F32)


def iota(shape, dim):
    return lax.broadcasted_iota(I32, shape, dim)


def to_row(col):
    n = col.shape[0]
    eye = iota((n, n), 0) == iota((n, n), 1)
    return jnp.sum(jnp.where(eye, col, jnp.zeros_like(col)), 0, keepdims=True)


def to_col(row):
    n = row.shape[1]
    eye = iota((n, n), 0) == iota((n, n), 1)
    return jnp.sum(jnp.where(eye, row, jnp.zeros_like(row)), 1, keepdims=True)


def one_hot(cond):
    return jnp.where(cond, 1.0, 0.0).astype(BF16)


def loop(n, body):
    lax.fori_loop(0, n, lambda t, carry: (body(t), carry)[1], 0)


def message_rows(n_msg, who, c):
    t, i = iota((n_msg, who.shape[1]), 0), iota((n_msg, who.shape[1]), 1)
    return one_hot(
        (lax.shift_right_logical(t, 4) == who)
        & (lax.bitwise_and(lax.shift_right_logical(t, 2), 3) == c)
        & (lax.bitwise_and(t, 3) == lax.bitwise_and(i, 3))
    )


def query_rows(n_msg, who, c):
    i, t = iota((who.shape[0], n_msg), 0), iota((who.shape[0], n_msg), 1)
    return one_hot(
        (lax.shift_right_logical(t, 4) == who)
        & (lax.bitwise_and(lax.shift_right_logical(t, 2), 3) == c)
        & (lax.bitwise_and(t, 3) == lax.bitwise_and(i, 3))
    )


def exchange_kernel(
    n_dp, q_hbm, p_hbm, t_hbm, ids_hbm, counts_hbm, home_hbm,
    gp_ref, gq_ref, loss_ref,
    ids_ref, counts_ref, home_ref, qv, pv, tv, s_ref, e_ref, wt_ref, stats, ob, base, arecv, grecv,
    req_out, req_in, ret_out, ret_in, qr, sneg, times_ref, eneg, oneg, factors,
    st_out, st_in, lse_out, lse_in,
    local_sem, ag_s, ag_r, rs_s, rs_r, st_s, st_r, ls_s, ls_r,
    rq_s, rq_r, rt_s, rt_r, group_there, peers_there,
):
    qd, d = q_hbm.shape
    pd = p_hbm.shape[0]
    half, piece = qd // 2, d // PIECES
    sub = half // SUBS
    slots = ids_ref.shape[0]
    n_msg = n_dp * 16
    nx = 4
    dp, me = lax.axis_index("dp"), lax.axis_index("blk")
    right = (dp, lax.rem(me + 1, nx))
    left = (dp, lax.rem(me + nx - 1, nx))
    across = (dp, lax.rem(me + 2, nx))

    barrier = pltpu.get_barrier_semaphore()
    first_plane = me == 0
    plane = jnp.maximum(me, 1)

    @pl.when(me != 0)
    def _():
        pl.semaphore_signal(barrier, inc=1, device_id=(dp, 0), device_id_type=MESH)

    def greet(j):
        peer = lax.rem(dp + j + 1, n_dp)
        pl.semaphore_signal(barrier, inc=1, device_id=(peer, plane), device_id_type=MESH)

    loop(n_dp - 1, greet)
    small_in = [
        pltpu.make_async_copy(src, dst, local_sem.at[3 + i])
        for i, (src, dst) in enumerate(((ids_hbm, ids_ref), (counts_hbm, counts_ref), (home_hbm, home_ref)))
    ]
    for copy in small_in:
        copy.start()
    q_in = pltpu.make_async_copy(q_hbm, qv.at[pl.ds(0, qd)], local_sem.at[0])
    p_in = pltpu.make_async_copy(p_hbm, pv, local_sem.at[1])
    t_in = pltpu.make_async_copy(t_hbm, tv, local_sem.at[2])
    q_in.start()
    p_in.start()
    t_in.start()

    @pl.when(first_plane)
    def _():
        pl.semaphore_wait(barrier, nx - 1)
        for b in range(1, nx):
            pl.semaphore_signal(group_there, inc=1, device_id=(dp, b), device_id_type=MESH)

    @pl.when(me != 0)
    def _():
        pl.semaphore_wait(group_there, 1)


    def remote(src, dst, send, recv, peer):
        return pltpu.make_async_remote_copy(
            src_ref=src, dst_ref=dst, send_sem=send, recv_sem=recv, device_id=peer, device_id_type=MESH
        )

    def half_rows(block, part, k=0, n=half):
        return pl.ds(block * qd + part * half + k * sub, n)

    def gather_step(i, src, block, part, peer):
        return remote(src, qv.at[half_rows(block, part)], ag_s.at[i], ag_r.at[i], peer)

    own = [q_hbm.at[pl.ds(0, half)], q_hbm.at[pl.ds(half, half)]]
    ag_r1 = gather_step(0, own[0], 1, 0, right)
    ag_l1 = gather_step(1, own[1], 1, 1, left)
    ag_r2 = gather_step(2, own[1], 2, 1, right)
    ag_l2 = gather_step(3, own[0], 2, 0, left)
    ag_r3 = gather_step(4, qv.at[half_rows(1, 0)], 3, 0, right)
    ag_l3 = gather_step(5, qv.at[half_rows(1, 1)], 3, 1, left)
    for copy in (ag_r1, ag_l1, ag_r2, ag_l2):
        copy.start()

    for copy in small_in:
        copy.wait()
    ids, home = ids_ref[...], home_ref[...]
    book = jnp.concatenate([lax.shift_right_logical(home, 7), lax.bitwise_and(home, 127)], 1)
    book = book.astype(F32).T.astype(BF16)
    n_hi = home.shape[0]
    together = 4
    named_rows = []
    for k in range(0, slots, together):
        id_row = jnp.concatenate([ids[k + i : k + i + 1] for i in range(together)], 1)
        pick = one_hot(lax.shift_right_logical(id_row, 7) == iota((n_hi, together * qd), 0))
        found = nn(book, pick)
        found = found[:128] * 128.0 + found[128:]
        mine = lax.bitwise_and(id_row, 127) == iota((128, together * qd), 0)
        row = jnp.sum(jnp.where(mine, found, 0.0), 0, keepdims=True).astype(I32)
        named_rows += [row[:, i * qd : (i + 1) * qd] for i in range(together)]
    rows = jnp.zeros((slots, qd), I32)
    for k in range(slots):
        rows = jnp.where(iota((slots, qd), 0) == k, named_rows[k], rows)
    live = iota((slots, qd), 0) < counts_ref[...]
    place = lax.bitwise_and(rows, 1023)
    meta_hi = jnp.where(live, lax.shift_right_logical(place, 5), -1).astype(F32)
    meta_lo = lax.bitwise_and(place, 31).astype(F32)
    blank = jnp.zeros((META - slots, qd), F32)
    meta_hi = jnp.concatenate([meta_hi, blank], 0).astype(BF16)
    meta_lo = jnp.concatenate([meta_lo, blank], 0).astype(BF16)
    owner_row = lax.shift_right_logical(named_rows[0], 10)
    width = 512

    def fill(buf, mats, src):
        def body(t):
            at = pl.multiple_of(t * width, width)
            total = nn(mats[0], src[pl.ds(0, qd), pl.ds(at, width)])
            for c in range(1, PIECES):
                total += nn(mats[c], src[pl.ds(0, qd), pl.ds(pl.multiple_of(at + c * piece, width), width)])
            buf[:, pl.ds(at, width)] = total.astype(BF16)

        loop(piece // width, body)

    def deliver(out, inn, send, recv):
        def copy(j, frm):
            to = lax.rem(dp + j, n_dp)
            return remote(
                out.at[pl.ds(pl.multiple_of(to * 16, 16), 16)],
                inn.at[pl.ds(pl.multiple_of(frm * 16, 16), 16)],
                send.at[j], recv.at[j], (to, me),
            )

        def came(j):
            return copy(j, lax.rem(dp + n_dp - j, n_dp))

        def begin():
            loop(n_dp - 1, lambda j: copy(j + 1, dp).start())
            mine = pl.ds(pl.multiple_of(dp * 16, 16), 16)
            inn[mine, :] = out[mine, :]

        def arrived():
            loop(n_dp - 1, lambda j: came(j + 1).wait_recv())

        def sent():
            loop(n_dp - 1, lambda j: came(j + 1).wait_send())

        return begin, arrived, sent

    request, request_in, request_sent = deliver(req_out, req_in, rq_s, rq_r)
    answer, answer_in, answer_sent = deliver(ret_out, ret_in, rt_s, rt_r)

    q_in.wait()
    pack = [message_rows(n_msg, owner_row, c) for c in range(PIECES)]
    fill(req_out, pack, qv)
    req_out[:, piece:] = (nt(pack[0], meta_hi) + nt(pack[1], meta_lo)).astype(BF16)

    @pl.when(me == 1)
    def _():
        pl.semaphore_wait(barrier, 2 * (n_dp - 1))
        pl.semaphore_signal(peers_there, inc=1, device_id=(dp, 0), device_id_type=MESH)

    @pl.when(me > 1)
    def _():
        pl.semaphore_wait(barrier, n_dp - 1)

    @pl.when(first_plane)
    def _():
        pl.semaphore_wait(peers_there, 1)

    request()

    def scores(block):
        cols = pl.ds(block * qd, qd)
        s_ref[:, cols] = SCALE * nt(pv[...], qv[cols, :])
        s = s_ref[:, cols]
        top = jnp.max(s, 0, keepdims=True)
        e = jnp.exp(s - top)
        stats[block, 0:1, :] = top
        stats[block, 1:2, :] = jnp.sum(e, 0, keepdims=True)
        for j in range(pd // 128):
            e_ref[:, j * 128 : (j + 1) * 128] = e[j * 128 : (j + 1) * 128].T.astype(BF16)

    wide = 2048

    def sums(dst, at):
        def body(t):
            cols = pl.ds(pl.multiple_of(t * wide, wide), wide)
            dst[pl.ds(at, qd), cols] = nn(e_ref[...], pv[:, cols]).astype(dst.dtype)

        loop(d // wide, body)

    p_in.wait()
    scores(0)
    sums(base, 0)

    ag_r1.wait_recv()
    ag_r3.start()
    ag_l1.wait_recv()
    ag_l3.start()
    scores(1)
    sums(ob, 0)

    request_in()
    t_in.wait()
    asker = lax.shift_right_logical(iota((qd, 1), 0), 2)
    for c in range(PIECES):
        qr[:, c * piece : (c + 1) * piece] = nn(query_rows(n_msg, asker, c), req_in[:, :piece]).astype(BF16)
    asker = lax.shift_right_logical(iota((1, qd), 1), 2)
    back = [message_rows(n_msg, asker, c) for c in range(PIECES)]
    tail = req_in[:, piece:]
    places = tn(tail, back[0]) * 32.0 + tn(tail, back[1])
    sneg[...] = SCALE * nt(tv[...], qr[...])
    n_rows = tv.shape[0]

    def neg_top(t, top):
        at = pl.ds(pl.multiple_of(t * 128, 128), 128)
        index = (iota((128, qd), 0) + t * 128).astype(F32)
        times = jnp.zeros((128, qd), F32)
        for k in range(slots):
            times += jnp.where(places[k : k + 1] == index, 1.0, 0.0)
        times_ref[at, :] = times
        return jnp.maximum(top, jnp.max(jnp.where(times > 0.0, sneg[at, :], -jnp.inf), 0, keepdims=True))

    m_far = lax.fori_loop(0, n_rows // 128, neg_top, jnp.full((1, qd), -jnp.inf, F32))

    def neg_weights(t, total):
        at = pl.ds(pl.multiple_of(t * 128, 128), 128)
        times = times_ref[at, :]
        e = jnp.where(times > 0.0, times * jnp.exp(jnp.minimum(sneg[at, :] - m_far, 0.0)), 0.0)
        eneg[:, at] = e.T.astype(BF16)
        return total + jnp.sum(e, 0, keepdims=True)

    l_far = lax.fori_loop(0, n_rows // 128, neg_weights, jnp.zeros((1, qd), F32))

    def neg_sums(t):
        cols = pl.ds(pl.multiple_of(t * wide, wide), wide)
        oneg[:, cols] = nn(eneg[...], tv[:, cols]).astype(BF16)

    loop(d // wide, neg_sums)
    fill(ret_out, back, oneg)
    line = iota((META, qd), 0)
    rest = jnp.where(line == 0, m_far, jnp.where(line == 1, l_far, 0.0))
    tail = jnp.zeros((n_msg, META), F32)
    for c in range(3):
        part = rest.astype(BF16)
        rest = rest - part.astype(F32)
        tail += nt(back[c], part)
    ret_out[:, piece:] = tail.astype(BF16)
    answer()

    ag_r2.wait_recv()
    ag_l2.wait_recv()
    scores(2)
    sums(ob, qd)

    def back_step(i, block, part, k, n, dst, at, peer):
        src = ob.at[half_rows(block - 1, part, k, n)]
        return remote(src, dst.at[pl.ds(at, n)], rs_s.at[i], rs_r.at[i], peer)

    both, quarter = 2, half // 2
    b_r = [back_step(k, 1, 1, k * SUBS // 2, quarter, grecv.at[0], half + k * quarter, right) for k in range(both)]
    b_l = [back_step(2 + k, 1, 0, k * SUBS // 2, quarter, grecv.at[1], k * quarter, left) for k in range(both)]
    a_r = [back_step(4 + 4 * k, 3, 0, k, sub, arecv.at[0], k * sub, right) for k in range(SUBS)]
    a_l = [back_step(5 + 4 * k, 3, 1, k, sub, arecv.at[1], k * sub, left) for k in range(SUBS)]
    c_r = [back_step(6 + 4 * k, 2, 0, k, sub, grecv.at[0], k * sub, right) for k in range(SUBS)]
    c_l = [back_step(7 + 4 * k, 2, 1, k, sub, grecv.at[1], half + k * sub, left) for k in range(SUBS)]
    b_r[0].start()
    b_l[0].start()
    ag_r3.wait_recv()
    ag_l3.wait_recv()
    scores(3)

    first = iota((8, qd), 1) < half
    picks = [stats[block, :, :] for block in range(nx)]
    st_out[0, :, :] = jnp.where(first, picks[2], picks[1])
    st_out[1, :, :] = picks[3]
    st_out[2, :, :] = jnp.where(first, picks[1], picks[2])
    st_out[3, :, :] = picks[3]
    st_right = remote(st_out.at[pl.ds(0, 2)], st_in.at[pl.ds(0, 2)], st_s.at[0], st_r.at[0], right)
    st_left = remote(st_out.at[pl.ds(2, 2)], st_in.at[pl.ds(2, 2)], st_s.at[1], st_r.at[1], left)
    st_across = remote(st_out.at[pl.ds(1, 1)], st_in.at[pl.ds(4, 1)], st_s.at[2], st_r.at[2], across)
    st_copies = [st_right, st_left, st_across]
    for copy in st_copies:
        copy.start()
    sums(ob, 2 * qd)
    for k in range(SUBS):
        a_r[k].start()
        a_l[k].start()

    answer_in()
    tail = ret_in[:, piece:]
    neg_stats = tn(tail, pack[0]) + tn(tail, pack[1]) + tn(tail, pack[2])
    for copy in st_copies:
        copy.wait_recv()

    def stat(entry, i):
        return st_in[entry, i : i + 1, :]

    m_own, l_own = stats[0, 0:1, :], stats[0, 1:2, :]
    m_l, l_l, m_r, l_r, m_x, l_x = (stat(e, i) for e in (0, 2, 4) for i in (0, 1))
    m_n, l_n = neg_stats[0:1], neg_stats[1:2]
    pairs = ((m_own, l_own), (m_l, l_l), (m_r, l_r), (m_x, l_x), (m_n, l_n))
    top = functools.reduce(jnp.maximum, [m for m, _ in pairs])
    lse = top + jnp.log(sum(l * jnp.exp(m - top) for m, l in pairs))
    lse_out[...] = jnp.broadcast_to(lse, (8, qd))
    lse_copies = [
        remote(lse_out, lse_in.at[i], ls_s.at[i], ls_r.at[i], peer)
        for i, peer in enumerate((right, left, across))
    ]
    for copy in lse_copies:
        copy.start()
    eye = iota((qd, qd), 0) == iota((qd, qd), 1)
    loss_ref[...] = lse - jnp.sum(jnp.where(eye, s_ref[pl.ds(0, qd), pl.ds(0, qd)], 0.0), 0, keepdims=True)

    f_own, f_n = to_col(jnp.exp(m_own - lse)), to_col(jnp.exp(m_n - lse))
    owner_col = to_col(owner_row)
    for c in range(PIECES):
        cols = pl.ds(c * piece, piece)
        neg = nn(query_rows(n_msg, owner_col, c), ret_in[:, :piece])
        base[:, cols] = f_own * base[:, cols] + f_n * neg - pv[pl.ds(0, qd), cols].astype(F32)

    for copy in lse_copies:
        copy.wait_recv()
    front = iota((1, qd), 1) < half
    lse_l, lse_r, lse_x = (lse_in[i, 0:1, :] for i in range(3))
    by_block = (lse, jnp.where(front, lse_l, lse_r), jnp.where(front, lse_r, lse_l), lse_x)
    for block in range(nx):
        cols = pl.ds(block * qd, qd)
        wt_ref[:, cols] = jnp.exp(s_ref[:, cols] - by_block[block]).astype(BF16)
    m_near = stats[2, 0:1, :]
    m_away = jnp.where(front, stat(1, 0), stat(3, 0))
    m_both = jnp.maximum(m_near, m_away)
    factors[0, :, :] = jnp.broadcast_to(to_col(jnp.exp(m_near - m_both)), (qd, 128))
    factors[1, :, :] = jnp.broadcast_to(to_col(jnp.exp(m_away - m_both)), (qd, 128))

    def merge(part, k):
        at, far_at = part * half + k * sub, pl.ds(k * sub, sub)
        f_near, f_away = factors[0, pl.ds(at, sub), :1], factors[1, pl.ds(at, sub), :1]

        def body(t):
            cols = pl.ds(pl.multiple_of(t * 1024, 1024), 1024)
            here = ob[pl.ds(qd + at, sub), cols].astype(F32)
            total = f_near * here + f_away * arecv[part, far_at, cols].astype(F32)
            ob[pl.ds(qd + at, sub), cols] = total.astype(BF16)

        loop(d // 1024, body)

    for k in range(SUBS):
        a_r[k].wait_send()
        a_l[k].wait_send()
    b_r[1].start()
    b_l[1].start()
    for k in range(SUBS):
        a_r[k].wait_recv()
        merge(0, k)
        c_r[k].start()
        a_l[k].wait_recv()
        merge(1, k)
        c_l[k].start()

    span = 1024

    def passage_grads(t):
        cols = pl.ds(pl.multiple_of(t * span, span), span)
        total = nn(wt_ref[...], qv[:, cols])
        gp_ref[pl.ds(qd, pd - qd), cols] = (SCALE * total[qd:]).astype(BF16)
        gp_ref[pl.ds(0, qd), cols] = (SCALE * (total[:qd] - qv[pl.ds(0, qd), cols].astype(F32))).astype(BF16)

    loop(d // span, passage_grads)

    request_sent()
    answer_sent()

    top_l, top_r = jnp.maximum(m_l, m_x), jnp.maximum(m_r, m_x)
    factors[2, :, :] = jnp.broadcast_to(to_col(jnp.exp(jnp.where(front, top_l, m_l) - lse)), (qd, 128))
    factors[3, :, :] = jnp.broadcast_to(to_col(jnp.exp(jnp.where(front, m_r, top_r) - lse)), (qd, 128))

    def finish(at):
        f_l, f_r = factors[2, pl.ds(at, sub), :1], factors[3, pl.ds(at, sub), :1]

        def body(t):
            cols = pl.ds(pl.multiple_of(t * 1024, 1024), 1024)
            total = base[pl.ds(at, sub), cols]
            total += f_l * grecv[0, pl.ds(at, sub), cols].astype(F32)
            total += f_r * grecv[1, pl.ds(at, sub), cols].astype(F32)
            gq_ref[pl.ds(at, sub), cols] = (SCALE * total).astype(BF16)

        loop(d // 1024, body)

    for copy in b_r + b_l:
        copy.wait_recv()
    for k in range(SUBS):
        c_r[k].wait_recv()
        finish(k * sub)
        c_l[k].wait_recv()
        finish(half + k * sub)

    for copy in [ag_r1, ag_r2, ag_r3, ag_l1, ag_l2, ag_l3] + b_r + b_l + c_r + c_l + st_copies + lse_copies:
        copy.wait_send()


def write_kernel(gp_in, gq_in, loss_in, gp_out, gq_out, loss_out, sems):
    parts = 4
    n = gp_in.shape[0] // parts
    copies = [
        pltpu.make_async_copy(gp_in.at[pl.ds(i * n, n)], gp_out.at[pl.ds(i * n, n)], sems.at[i]) for i in range(parts)
    ]
    copies.append(pltpu.make_async_copy(gq_in, gq_out, sems.at[parts]))
    copies.append(pltpu.make_async_copy(loss_in, loss_out, sems.at[parts + 1]))
    for copy in copies:
        copy.start()
    for copy in copies:
        copy.wait()


def per_device(n_dp, queries, passages, neg_table, neg_ids, counts, neg_home):
    qd, d = queries.shape
    pd = passages.shape[0]
    n_rows = neg_table.shape[0]
    nx, half = 4, qd // 2
    n_msg, piece = n_dp * 16, d // PIECES
    any_spec = pl.BlockSpec(memory_space=pl.ANY)
    vmem_spec = pl.BlockSpec(memory_space=pltpu.VMEM)
    dma = pltpu.SemaphoreType.DMA
    grad_p, grad_q, loss = pl.pallas_call(
        functools.partial(exchange_kernel, n_dp),
        out_shape=(
            pltpu.VMEM((pd, d), BF16),
            pltpu.VMEM((qd, d), BF16),
            pltpu.VMEM((1, qd), F32),
        ),
        in_specs=[any_spec] * 6,
        out_specs=(vmem_spec, vmem_spec, vmem_spec),
        scratch_shapes=[
            pltpu.VMEM(neg_ids.T.shape, I32),
            pltpu.VMEM((1, qd), I32),
            pltpu.VMEM((neg_home.shape[0] // 128, 128), I32),
            pltpu.VMEM((nx * qd, d), BF16),
            pltpu.VMEM((pd, d), BF16),
            pltpu.VMEM((n_rows, d), BF16),
            pltpu.VMEM((pd, nx * qd), F32),
            pltpu.VMEM((qd, pd), BF16),
            pltpu.VMEM((pd, nx * qd), BF16),
            pltpu.VMEM((nx, 8, qd), F32),
            pltpu.VMEM(((nx - 1) * qd, d), BF16),
            pltpu.VMEM((qd, d), F32),
            pltpu.VMEM((2, half, d), BF16),
            pltpu.VMEM((2, qd, d), BF16),
            pltpu.VMEM((n_msg, piece + META), BF16),
            pltpu.VMEM((n_msg, piece + META), BF16),
            pltpu.VMEM((n_msg, piece + META), BF16),
            pltpu.VMEM((n_msg, piece + META), BF16),
            pltpu.VMEM((qd, d), BF16),
            pltpu.VMEM((n_rows, qd), F32),
            pltpu.VMEM((n_rows, qd), F32),
            pltpu.VMEM((qd, n_rows), BF16),
            pltpu.VMEM((qd, d), BF16),
            pltpu.VMEM((4, qd, 128), F32),
            pltpu.VMEM((4, 8, qd), F32),
            pltpu.VMEM((5, 8, qd), F32),
            pltpu.VMEM((8, qd), F32),
            pltpu.VMEM((3, 8, qd), F32),
            dma((6,)),
            dma((6,)),
            dma((6,)),
            dma((4 + 4 * SUBS,)),
            dma((4 + 4 * SUBS,)),
            dma((3,)),
            dma((3,)),
            dma((3,)),
            dma((3,)),
            dma((n_dp,)),
            dma((n_dp,)),
            dma((n_dp,)),
            dma((n_dp,)),
            pltpu.SemaphoreType.REGULAR,
            pltpu.SemaphoreType.REGULAR,
        ],
        compiler_params=pltpu.CompilerParams(
            collective_id=0, has_side_effects=True, vmem_limit_bytes=54 * 1024 * 1024
        ),
        cost_estimate=pl.CostEstimate(flops=13_000_000_000, bytes_accessed=25_000_000, transcendentals=1_000_000),
        name="exchange",
    )(queries, passages, neg_table, neg_ids.T, counts.reshape(1, qd), neg_home.reshape(-1, 128))
    grad_p, grad_q, loss = pl.pallas_call(
        write_kernel,
        out_shape=(
            jax.ShapeDtypeStruct((pd, d), BF16),
            jax.ShapeDtypeStruct((qd, d), BF16),
            jax.ShapeDtypeStruct((1, qd), F32),
        ),
        in_specs=[any_spec] * 3,
        out_specs=(any_spec, any_spec, any_spec),
        scratch_shapes=[dma((6,))],
        compiler_params=pltpu.CompilerParams(vmem_limit_bytes=1024 * 1024),
        cost_estimate=pl.CostEstimate(flops=0, bytes_accessed=7_300_000, transcendentals=0),
        name="write",
    )(grad_p, grad_q, loss)
    return loss.reshape(qd), grad_q, grad_p


def solution(mesh):
    in_specs = (
        P(("dp", "blk"), None),
        P(("dp", "blk"), None),
        P("dp", None),
        P(("dp", "blk"), None),
        P(("dp", "blk")),
        P(),
    )
    out_specs = (P(("dp", "blk")), P(("dp", "blk"), None), P(("dp", "blk"), None))
    return jax.shard_map(
        functools.partial(per_device, mesh.shape["dp"]),
        mesh=mesh, in_specs=in_specs, out_specs=out_specs, check_vma=False,
    )
```

```python
import functools

import jax
import jax.numpy as jnp
from jax import lax
from jax.experimental import pallas as pl
from jax.experimental.pallas import tpu as pltpu
from jax.sharding import PartitionSpec as P

MESH = pl.DeviceIdType.MESH
F32, BF16, I32 = jnp.float32, jnp.bfloat16, jnp.int32
SCALE = 0.0625
META = 128
PIECES = 4
SUBS = 4


def nn(a, b):
    return jnp.dot(a, b, preferred_element_type=F32)


def nt(a, b):
    return lax.dot_general(a, b, (((1,), (1,)), ((), ())), preferred_element_type=F32)


def tn(a, b):
    return lax.dot_general(a, b, (((0,), (0,)), ((), ())), preferred_element_type=F32)


def iota(shape, dim):
    return lax.broadcasted_iota(I32, shape, dim)


def to_row(col):
    n = col.shape[0]
    eye = iota((n, n), 0) == iota((n, n), 1)
    return jnp.sum(jnp.where(eye, col, jnp.zeros_like(col)), 0, keepdims=True)


def to_col(row):
    n = row.shape[1]
    eye = iota((n, n), 0) == iota((n, n), 1)
    return jnp.sum(jnp.where(eye, row, jnp.zeros_like(row)), 1, keepdims=True)


def one_hot(cond):
    return jnp.where(cond, 1.0, 0.0).astype(BF16)


def loop(n, body):
    lax.fori_loop(0, n, lambda t, carry: (body(t), carry)[1], 0)


def message_rows(n_msg, who, c):
    t, i = iota((n_msg, who.shape[1]), 0), iota((n_msg, who.shape[1]), 1)
    return one_hot(
        (lax.shift_right_logical(t, 4) == who)
        & (lax.bitwise_and(lax.shift_right_logical(t, 2), 3) == c)
        & (lax.bitwise_and(t, 3) == lax.bitwise_and(i, 3))
    )


def query_rows(n_msg, who, c):
    i, t = iota((who.shape[0], n_msg), 0), iota((who.shape[0], n_msg), 1)
    return one_hot(
        (lax.shift_right_logical(t, 4) == who)
        & (lax.bitwise_and(lax.shift_right_logical(t, 2), 3) == c)
        & (lax.bitwise_and(t, 3) == lax.bitwise_and(i, 3))
    )


def exchange_kernel(
    n_dp, q_hbm, p_hbm, t_hbm, ids_hbm, counts_hbm, home_hbm,
    gp_ref, gq_ref, loss_ref,
    ids_ref, counts_ref, home_ref, qv, pv, tv, s_ref, e_ref, wt_ref, stats, ob, base, arecv, grecv,
    req_out, req_in, ret_out, ret_in, qr, sneg, times_ref, eneg, oneg, factors,
    st_out, st_in, lse_out, lse_in,
    local_sem, ag_s, ag_r, rs_s, rs_r, st_s, st_r, ls_s, ls_r,
    rq_s, rq_r, rt_s, rt_r, group_there, peers_there,
):
    qd, d = q_hbm.shape
    pd = p_hbm.shape[0]
    half, piece = qd // 2, d // PIECES
    sub = half // SUBS
    slots = ids_ref.shape[0]
    n_msg = n_dp * 16
    nx = 4
    dp, me = lax.axis_index("dp"), lax.axis_index("blk")
    right = (dp, lax.rem(me + 1, nx))
    left = (dp, lax.rem(me + nx - 1, nx))
    across = (dp, lax.rem(me + 2, nx))

    barrier = pltpu.get_barrier_semaphore()
    first_plane = me == 0
    plane = jnp.maximum(me, 1)

    @pl.when(me != 0)
    def _():
        pl.semaphore_signal(barrier, inc=1, device_id=(dp, 0), device_id_type=MESH)

    def greet(j):
        peer = lax.rem(dp + j + 1, n_dp)
        pl.semaphore_signal(barrier, inc=1, device_id=(peer, plane), device_id_type=MESH)

    loop(n_dp - 1, greet)
    small_in = [
        pltpu.make_async_copy(src, dst, local_sem.at[3 + i])
        for i, (src, dst) in enumerate(((ids_hbm, ids_ref), (counts_hbm, counts_ref), (home_hbm, home_ref)))
    ]
    for copy in small_in:
        copy.start()
    q_in = pltpu.make_async_copy(q_hbm, qv.at[pl.ds(0, qd)], local_sem.at[0])
    p_in = pltpu.make_async_copy(p_hbm, pv, local_sem.at[1])
    t_in = pltpu.make_async_copy(t_hbm, tv, local_sem.at[2])
    q_in.start()
    p_in.start()
    t_in.start()

    @pl.when(first_plane)
    def _():
        pl.semaphore_wait(barrier, nx - 1)
        for b in range(1, nx):
            pl.semaphore_signal(group_there, inc=1, device_id=(dp, b), device_id_type=MESH)

    @pl.when(me != 0)
    def _():
        pl.semaphore_wait(group_there, 1)


    def remote(src, dst, send, recv, peer):
        return pltpu.make_async_remote_copy(
            src_ref=src, dst_ref=dst, send_sem=send, recv_sem=recv, device_id=peer, device_id_type=MESH
        )

    def half_rows(block, part, k=0, n=half):
        return pl.ds(block * qd + part * half + k * sub, n)

    def gather_step(i, src, block, part, peer):
        return remote(src, qv.at[half_rows(block, part)], ag_s.at[i], ag_r.at[i], peer)

    own = [q_hbm.at[pl.ds(0, half)], q_hbm.at[pl.ds(half, half)]]
    ag_r1 = gather_step(0, own[0], 1, 0, right)
    ag_l1 = gather_step(1, own[1], 1, 1, left)
    ag_r2 = gather_step(2, own[1], 2, 1, right)
    ag_l2 = gather_step(3, own[0], 2, 0, left)
    ag_r3 = gather_step(4, qv.at[half_rows(1, 0)], 3, 0, right)
    ag_l3 = gather_step(5, qv.at[half_rows(1, 1)], 3, 1, left)
    for copy in (ag_r1, ag_l1, ag_r2, ag_l2):
        copy.start()

    for copy in small_in:
        copy.wait()
    ids, home = ids_ref[...], home_ref[...]
    book = jnp.concatenate([lax.shift_right_logical(home, 7), lax.bitwise_and(home, 127)], 1)
    book = book.astype(F32).T.astype(BF16)
    n_hi = home.shape[0]
    together = 4
    named_rows = []
    for k in range(0, slots, together):
        id_row = jnp.concatenate([ids[k + i : k + i + 1] for i in range(together)], 1)
        pick = one_hot(lax.shift_right_logical(id_row, 7) == iota((n_hi, together * qd), 0))
        found = nn(book, pick)
        found = found[:128] * 128.0 + found[128:]
        mine = lax.bitwise_and(id_row, 127) == iota((128, together * qd), 0)
        row = jnp.sum(jnp.where(mine, found, 0.0), 0, keepdims=True).astype(I32)
        named_rows += [row[:, i * qd : (i + 1) * qd] for i in range(together)]
    rows = jnp.zeros((slots, qd), I32)
    for k in range(slots):
        rows = jnp.where(iota((slots, qd), 0) == k, named_rows[k], rows)
    live = iota((slots, qd), 0) < counts_ref[...]
    place = lax.bitwise_and(rows, 1023)
    meta_hi = jnp.where(live, lax.shift_right_logical(place, 5), -1).astype(F32)
    meta_lo = lax.bitwise_and(place, 31).astype(F32)
    blank = jnp.zeros((META - slots, qd), F32)
    meta_hi = jnp.concatenate([meta_hi, blank], 0).astype(BF16)
    meta_lo = jnp.concatenate([meta_lo, blank], 0).astype(BF16)
    owner_row = lax.shift_right_logical(named_rows[0], 10)
    width = 512

    def fill(buf, mats, src):
        def body(t):
            at = pl.multiple_of(t * width, width)
            total = nn(mats[0], src[pl.ds(0, qd), pl.ds(at, width)])
            for c in range(1, PIECES):
                total += nn(mats[c], src[pl.ds(0, qd), pl.ds(pl.multiple_of(at + c * piece, width), width)])
            buf[:, pl.ds(at, width)] = total.astype(BF16)

        loop(piece // width, body)

    def deliver(out, inn, send, recv):
        def copy(j, frm):
            to = lax.rem(dp + j, n_dp)
            return remote(
                out.at[pl.ds(pl.multiple_of(to * 16, 16), 16)],
                inn.at[pl.ds(pl.multiple_of(frm * 16, 16), 16)],
                send.at[0], recv.at[0], (to, me),
            )

        every = pl.ds(0, (n_dp - 1) * 16)
        whole = remote(out.at[every], inn.at[every], send.at[0], recv.at[0], right)

        def begin():
            loop(n_dp - 1, lambda j: copy(j + 1, dp).start())
            mine = pl.ds(pl.multiple_of(dp * 16, 16), 16)
            inn[mine, :] = out[mine, :]

        def arrived():
            whole.wait_recv()

        def sent():
            whole.wait_send()

        return begin, arrived, sent

    request, request_in, request_sent = deliver(req_out, req_in, rq_s, rq_r)
    answer, answer_in, answer_sent = deliver(ret_out, ret_in, rt_s, rt_r)

    q_in.wait()
    pack = [message_rows(n_msg, owner_row, c) for c in range(PIECES)]
    fill(req_out, pack, qv)
    req_out[:, piece:] = (nt(pack[0], meta_hi) + nt(pack[1], meta_lo)).astype(BF16)

    def scores(block):
        cols = pl.ds(block * qd, qd)
        s_ref[:, cols] = SCALE * nt(pv[...], qv[cols, :])
        s = s_ref[:, cols]
        top = jnp.max(s, 0, keepdims=True)
        e = jnp.exp(s - top)
        stats[block, 0:1, :] = top
        stats[block, 1:2, :] = jnp.sum(e, 0, keepdims=True)
        for j in range(pd // 128):
            e_ref[:, j * 128 : (j + 1) * 128] = e[j * 128 : (j + 1) * 128].T.astype(BF16)

    wide = 2048

    def sums(dst, at):
        def body(t):
            cols = pl.ds(pl.multiple_of(t * wide, wide), wide)
            dst[pl.ds(at, qd), cols] = nn(e_ref[...], pv[:, cols]).astype(dst.dtype)

        loop(d // wide, body)

    p_in.wait()
    scores(0)
    sums(base, 0)
    @pl.when(me == 1)
    def _():
        pl.semaphore_wait(barrier, 2 * (n_dp - 1))
        pl.semaphore_signal(peers_there, inc=1, device_id=(dp, 0), device_id_type=MESH)

    @pl.when(me > 1)
    def _():
        pl.semaphore_wait(barrier, n_dp - 1)

    @pl.when(first_plane)
    def _():
        pl.semaphore_wait(peers_there, 1)

    request()

    ag_r1.wait_recv()
    ag_r3.start()
    ag_l1.wait_recv()
    ag_l3.start()
    scores(1)
    sums(ob, 0)

    ag_r2.wait_recv()
    ag_l2.wait_recv()
    scores(2)
    sums(ob, qd)

    def back_step(i, block, part, k, n, dst, at, peer):
        src = ob.at[half_rows(block - 1, part, k, n)]
        return remote(src, dst.at[pl.ds(at, n)], rs_s.at[i], rs_r.at[i], peer)

    both, quarter = 2, half // 2
    b_r = [back_step(k, 1, 1, k * SUBS // 2, quarter, grecv.at[0], half + k * quarter, right) for k in range(both)]
    b_l = [back_step(2 + k, 1, 0, k * SUBS // 2, quarter, grecv.at[1], k * quarter, left) for k in range(both)]
    a_r = [back_step(4 + 4 * k, 3, 0, k, sub, arecv.at[0], k * sub, right) for k in range(SUBS)]
    a_l = [back_step(5 + 4 * k, 3, 1, k, sub, arecv.at[1], k * sub, left) for k in range(SUBS)]
    c_r = [back_step(6 + 4 * k, 2, 0, k, sub, grecv.at[0], k * sub, right) for k in range(SUBS)]
    c_l = [back_step(7 + 4 * k, 2, 1, k, sub, grecv.at[1], half + k * sub, left) for k in range(SUBS)]
    for copy in b_r + b_l:
        copy.start()
    request_in()
    t_in.wait()
    asker = lax.shift_right_logical(iota((qd, 1), 0), 2)
    for c in range(PIECES):
        qr[:, c * piece : (c + 1) * piece] = nn(query_rows(n_msg, asker, c), req_in[:, :piece]).astype(BF16)
    asker = lax.shift_right_logical(iota((1, qd), 1), 2)
    back = [message_rows(n_msg, asker, c) for c in range(PIECES)]
    tail = req_in[:, piece:]
    places = tn(tail, back[0]) * 32.0 + tn(tail, back[1])
    sneg[...] = SCALE * nt(tv[...], qr[...])
    n_rows = tv.shape[0]

    def neg_top(t, top):
        at = pl.ds(pl.multiple_of(t * 128, 128), 128)
        index = (iota((128, qd), 0) + t * 128).astype(F32)
        times = jnp.zeros((128, qd), F32)
        for k in range(slots):
            times += jnp.where(places[k : k + 1] == index, 1.0, 0.0)
        times_ref[at, :] = times
        return jnp.maximum(top, jnp.max(jnp.where(times > 0.0, sneg[at, :], -jnp.inf), 0, keepdims=True))

    m_far = lax.fori_loop(0, n_rows // 128, neg_top, jnp.full((1, qd), -jnp.inf, F32))

    def neg_weights(t, total):
        at = pl.ds(pl.multiple_of(t * 128, 128), 128)
        times = times_ref[at, :]
        e = jnp.where(times > 0.0, times * jnp.exp(jnp.minimum(sneg[at, :] - m_far, 0.0)), 0.0)
        eneg[:, at] = e.T.astype(BF16)
        return total + jnp.sum(e, 0, keepdims=True)

    l_far = lax.fori_loop(0, n_rows // 128, neg_weights, jnp.zeros((1, qd), F32))

    def neg_sums(t):
        cols = pl.ds(pl.multiple_of(t * wide, wide), wide)
        oneg[:, cols] = nn(eneg[...], tv[:, cols]).astype(BF16)

    loop(d // wide, neg_sums)
    fill(ret_out, back, oneg)
    line = iota((META, qd), 0)
    rest = jnp.where(line == 0, m_far, jnp.where(line == 1, l_far, 0.0))
    tail = jnp.zeros((n_msg, META), F32)
    for c in range(3):
        part = rest.astype(BF16)
        rest = rest - part.astype(F32)
        tail += nt(back[c], part)
    ret_out[:, piece:] = tail.astype(BF16)
    answer()

    ag_r3.wait_recv()
    ag_l3.wait_recv()
    scores(3)

    first = iota((8, qd), 1) < half
    picks = [stats[block, :, :] for block in range(nx)]
    st_out[0, :, :] = jnp.where(first, picks[2], picks[1])
    st_out[1, :, :] = picks[3]
    st_out[2, :, :] = jnp.where(first, picks[1], picks[2])
    st_out[3, :, :] = picks[3]
    st_right = remote(st_out.at[pl.ds(0, 2)], st_in.at[pl.ds(0, 2)], st_s.at[0], st_r.at[0], right)
    st_left = remote(st_out.at[pl.ds(2, 2)], st_in.at[pl.ds(2, 2)], st_s.at[1], st_r.at[1], left)
    st_across = remote(st_out.at[pl.ds(1, 1)], st_in.at[pl.ds(4, 1)], st_s.at[2], st_r.at[2], across)
    st_copies = [st_right, st_left, st_across]
    for copy in st_copies:
        copy.start()
    sums(ob, 2 * qd)
    for k in range(SUBS):
        a_r[k].start()
        a_l[k].start()

    answer_in()
    tail = ret_in[:, piece:]
    neg_stats = tn(tail, pack[0]) + tn(tail, pack[1]) + tn(tail, pack[2])
    for copy in st_copies:
        copy.wait_recv()

    def stat(entry, i):
        return st_in[entry, i : i + 1, :]

    m_own, l_own = stats[0, 0:1, :], stats[0, 1:2, :]
    m_l, l_l, m_r, l_r, m_x, l_x = (stat(e, i) for e in (0, 2, 4) for i in (0, 1))
    m_n, l_n = neg_stats[0:1], neg_stats[1:2]
    pairs = ((m_own, l_own), (m_l, l_l), (m_r, l_r), (m_x, l_x), (m_n, l_n))
    top = functools.reduce(jnp.maximum, [m for m, _ in pairs])
    lse = top + jnp.log(sum(l * jnp.exp(m - top) for m, l in pairs))
    lse_out[...] = jnp.broadcast_to(lse, (8, qd))
    lse_copies = [
        remote(lse_out, lse_in.at[i], ls_s.at[i], ls_r.at[i], peer)
        for i, peer in enumerate((right, left, across))
    ]
    for copy in lse_copies:
        copy.start()
    eye = iota((qd, qd), 0) == iota((qd, qd), 1)
    loss_ref[...] = lse - jnp.sum(jnp.where(eye, s_ref[pl.ds(0, qd), pl.ds(0, qd)], 0.0), 0, keepdims=True)

    f_own, f_n = to_col(jnp.exp(m_own - lse)), to_col(jnp.exp(m_n - lse))
    owner_col = to_col(owner_row)
    for c in range(PIECES):
        cols = pl.ds(c * piece, piece)
        neg = nn(query_rows(n_msg, owner_col, c), ret_in[:, :piece])
        base[:, cols] = f_own * base[:, cols] + f_n * neg - pv[pl.ds(0, qd), cols].astype(F32)

    front = iota((1, qd), 1) < half

    m_near = stats[2, 0:1, :]
    m_away = jnp.where(front, stat(1, 0), stat(3, 0))
    m_both = jnp.maximum(m_near, m_away)
    factors[0, :, :] = jnp.broadcast_to(to_col(jnp.exp(m_near - m_both)), (qd, 128))
    factors[1, :, :] = jnp.broadcast_to(to_col(jnp.exp(m_away - m_both)), (qd, 128))

    def merge(part, k):
        at, far_at = part * half + k * sub, pl.ds(k * sub, sub)
        f_near, f_away = factors[0, pl.ds(at, sub), :1], factors[1, pl.ds(at, sub), :1]

        def body(t):
            cols = pl.ds(pl.multiple_of(t * 1024, 1024), 1024)
            here = ob[pl.ds(qd + at, sub), cols].astype(F32)
            total = f_near * here + f_away * arecv[part, far_at, cols].astype(F32)
            ob[pl.ds(qd + at, sub), cols] = total.astype(BF16)

        loop(d // 1024, body)

    for k in range(SUBS):
        a_r[k].wait_recv()
        merge(0, k)
        c_r[k].start()
        a_l[k].wait_recv()
        merge(1, k)
        c_l[k].start()

    for copy in lse_copies:
        copy.wait_recv()
    lse_l, lse_r, lse_x = (lse_in[i, 0:1, :] for i in range(3))
    by_block = (lse, jnp.where(front, lse_l, lse_r), jnp.where(front, lse_r, lse_l), lse_x)
    for block in range(nx):
        cols = pl.ds(block * qd, qd)
        wt_ref[:, cols] = jnp.exp(s_ref[:, cols] - by_block[block]).astype(BF16)
    span = 1024

    def passage_grads(t):
        cols = pl.ds(pl.multiple_of(t * span, span), span)
        total = nn(wt_ref[...], qv[:, cols])
        gp_ref[pl.ds(qd, pd - qd), cols] = (SCALE * total[qd:]).astype(BF16)
        gp_ref[pl.ds(0, qd), cols] = (SCALE * (total[:qd] - qv[pl.ds(0, qd), cols].astype(F32))).astype(BF16)

    loop(d // span, passage_grads)

    request_sent()
    answer_sent()

    top_l, top_r = jnp.maximum(m_l, m_x), jnp.maximum(m_r, m_x)
    factors[2, :, :] = jnp.broadcast_to(to_col(jnp.exp(jnp.where(front, top_l, m_l) - lse)), (qd, 128))
    factors[3, :, :] = jnp.broadcast_to(to_col(jnp.exp(jnp.where(front, m_r, top_r) - lse)), (qd, 128))

    def finish(at):
        f_l, f_r = factors[2, pl.ds(at, sub), :1], factors[3, pl.ds(at, sub), :1]

        def body(t):
            cols = pl.ds(pl.multiple_of(t * 1024, 1024), 1024)
            total = base[pl.ds(at, sub), cols]
            total += f_l * grecv[0, pl.ds(at, sub), cols].astype(F32)
            total += f_r * grecv[1, pl.ds(at, sub), cols].astype(F32)
            gq_ref[pl.ds(at, sub), cols] = (SCALE * total).astype(BF16)

        loop(d // 1024, body)

    for copy in b_r + b_l:
        copy.wait_recv()
    for k in range(SUBS):
        c_r[k].wait_recv()
        finish(k * sub)
        c_l[k].wait_recv()
        finish(half + k * sub)

    for copy in [ag_r1, ag_r2, ag_r3, ag_l1, ag_l2, ag_l3] + b_r + b_l + a_r + a_l + c_r + c_l + st_copies + lse_copies:
        copy.wait_send()


def write_kernel(gp_in, gq_in, loss_in, gp_out, gq_out, loss_out, sems):
    parts = 4
    n = gp_in.shape[0] // parts
    copies = [
        pltpu.make_async_copy(gp_in.at[pl.ds(i * n, n)], gp_out.at[pl.ds(i * n, n)], sems.at[i]) for i in range(parts)
    ]
    copies.append(pltpu.make_async_copy(gq_in, gq_out, sems.at[parts]))
    copies.append(pltpu.make_async_copy(loss_in, loss_out, sems.at[parts + 1]))
    for copy in copies:
        copy.start()
    for copy in copies:
        copy.wait()


def per_device(n_dp, queries, passages, neg_table, neg_ids, counts, neg_home):
    qd, d = queries.shape
    pd = passages.shape[0]
    n_rows = neg_table.shape[0]
    nx, half = 4, qd // 2
    n_msg, piece = n_dp * 16, d // PIECES
    any_spec = pl.BlockSpec(memory_space=pl.ANY)
    vmem_spec = pl.BlockSpec(memory_space=pltpu.VMEM)
    dma = pltpu.SemaphoreType.DMA
    grad_p, grad_q, loss = pl.pallas_call(
        functools.partial(exchange_kernel, n_dp),
        out_shape=(
            pltpu.VMEM((pd, d), BF16),
            pltpu.VMEM((qd, d), BF16),
            pltpu.VMEM((1, qd), F32),
        ),
        in_specs=[any_spec] * 6,
        out_specs=(vmem_spec, vmem_spec, vmem_spec),
        scratch_shapes=[
            pltpu.VMEM(neg_ids.T.shape, I32),
            pltpu.VMEM((1, qd), I32),
            pltpu.VMEM((neg_home.shape[0] // 128, 128), I32),
            pltpu.VMEM((nx * qd, d), BF16),
            pltpu.VMEM((pd, d), BF16),
            pltpu.VMEM((n_rows, d), BF16),
            pltpu.VMEM((pd, nx * qd), F32),
            pltpu.VMEM((qd, pd), BF16),
            pltpu.VMEM((pd, nx * qd), BF16),
            pltpu.VMEM((nx, 8, qd), F32),
            pltpu.VMEM(((nx - 1) * qd, d), BF16),
            pltpu.VMEM((qd, d), F32),
            pltpu.VMEM((2, half, d), BF16),
            pltpu.VMEM((2, qd, d), BF16),
            pltpu.VMEM((n_msg, piece + META), BF16),
            pltpu.VMEM((n_msg, piece + META), BF16),
            pltpu.VMEM((n_msg, piece + META), BF16),
            pltpu.VMEM((n_msg, piece + META), BF16),
            pltpu.VMEM((qd, d), BF16),
            pltpu.VMEM((n_rows, qd), F32),
            pltpu.VMEM((n_rows, qd), F32),
            pltpu.VMEM((qd, n_rows), BF16),
            pltpu.VMEM((qd, d), BF16),
            pltpu.VMEM((4, qd, 128), F32),
            pltpu.VMEM((4, 8, qd), F32),
            pltpu.VMEM((5, 8, qd), F32),
            pltpu.VMEM((8, qd), F32),
            pltpu.VMEM((3, 8, qd), F32),
            dma((6,)),
            dma((6,)),
            dma((6,)),
            dma((4 + 4 * SUBS,)),
            dma((4 + 4 * SUBS,)),
            dma((3,)),
            dma((3,)),
            dma((3,)),
            dma((3,)),
            dma((1,)),
            dma((1,)),
            dma((1,)),
            dma((1,)),
            pltpu.SemaphoreType.REGULAR,
            pltpu.SemaphoreType.REGULAR,
        ],
        compiler_params=pltpu.CompilerParams(
            collective_id=0, has_side_effects=True, vmem_limit_bytes=54 * 1024 * 1024
        ),
        cost_estimate=pl.CostEstimate(flops=13_000_000_000, bytes_accessed=25_000_000, transcendentals=1_000_000),
        name="exchange",
    )(queries, passages, neg_table, neg_ids.T, counts.reshape(1, qd), neg_home.reshape(-1, 128))
    grad_p, grad_q, loss = pl.pallas_call(
        write_kernel,
        out_shape=(
            jax.ShapeDtypeStruct((pd, d), BF16),
            jax.ShapeDtypeStruct((qd, d), BF16),
            jax.ShapeDtypeStruct((1, qd), F32),
        ),
        in_specs=[any_spec] * 3,
        out_specs=(any_spec, any_spec, any_spec),
        scratch_shapes=[dma((6,))],
        compiler_params=pltpu.CompilerParams(vmem_limit_bytes=1024 * 1024),
        cost_estimate=pl.CostEstimate(flops=0, bytes_accessed=7_300_000, transcendentals=0),
        name="write",
    )(grad_p, grad_q, loss)
    return loss.reshape(qd), grad_q, grad_p


def solution(mesh):
    in_specs = (
        P(("dp", "blk"), None),
        P(("dp", "blk"), None),
        P("dp", None),
        P(("dp", "blk"), None),
        P(("dp", "blk")),
        P(),
    )
    out_specs = (P(("dp", "blk")), P(("dp", "blk"), None), P(("dp", "blk"), None))
    return jax.shard_map(
        functools.partial(per_device, mesh.shape["dp"]),
        mesh=mesh, in_specs=in_specs, out_specs=out_specs, check_vma=False,
    )
```

```python
import functools

import jax
import jax.numpy as jnp
from jax import lax
from jax.experimental import pallas as pl
from jax.experimental.pallas import tpu as pltpu
from jax.sharding import PartitionSpec as P

MESH = pl.DeviceIdType.MESH
F32, BF16, I32 = jnp.float32, jnp.bfloat16, jnp.int32
SCALE = 0.0625
META = 128
PIECES = 4
SUBS = 2
HUB, AIDE = 2, 1


def nn(a, b):
    return jnp.dot(a, b, preferred_element_type=F32)


def nt(a, b):
    return lax.dot_general(a, b, (((1,), (1,)), ((), ())), preferred_element_type=F32)


def tn(a, b):
    return lax.dot_general(a, b, (((0,), (0,)), ((), ())), preferred_element_type=F32)


def iota(shape, dim):
    return lax.broadcasted_iota(I32, shape, dim)


def to_row(col):
    n = col.shape[0]
    eye = iota((n, n), 0) == iota((n, n), 1)
    return jnp.sum(jnp.where(eye, col, jnp.zeros_like(col)), 0, keepdims=True)


def to_col(row):
    n = row.shape[1]
    eye = iota((n, n), 0) == iota((n, n), 1)
    return jnp.sum(jnp.where(eye, row, jnp.zeros_like(row)), 1, keepdims=True)


def one_hot(cond):
    return jnp.where(cond, 1.0, 0.0).astype(BF16)


def loop(n, body):
    lax.fori_loop(0, n, lambda t, carry: (body(t), carry)[1], 0)


def message_rows(n_msg, who, c):
    t, i = iota((n_msg, who.shape[1]), 0), iota((n_msg, who.shape[1]), 1)
    return one_hot(
        (lax.shift_right_logical(t, 4) == who)
        & (lax.bitwise_and(lax.shift_right_logical(t, 2), 3) == c)
        & (lax.bitwise_and(t, 3) == lax.bitwise_and(i, 3))
    )


def query_rows(n_msg, who, c):
    i, t = iota((who.shape[0], n_msg), 0), iota((who.shape[0], n_msg), 1)
    return one_hot(
        (lax.shift_right_logical(t, 4) == who)
        & (lax.bitwise_and(lax.shift_right_logical(t, 2), 3) == c)
        & (lax.bitwise_and(t, 3) == lax.bitwise_and(i, 3))
    )


def exchange_kernel(
    n_dp, q_hbm, p_hbm, t_hbm, ids_hbm, counts_hbm, home_hbm,
    gp_ref, gq_ref, loss_ref,
    ids_ref, counts_ref, home_ref, qv, pv, tv, s_ref, e_ref, wt_ref, stats, ob, base, arecv, grecv,
    req_out, req_in, ret_out, ret_in, qr, sneg, times_ref, eneg, oneg, factors,
    st_out, st_in, lse_out, lse_in,
    local_sem, ag_s, ag_r, rs_s, rs_r, st_s, st_r, ls_s, ls_r,
    rq_s, rq_r, rt_s, rt_r, group_there, peers_there,
):
    qd, d = q_hbm.shape
    pd = p_hbm.shape[0]
    half, piece = qd // 2, d // PIECES
    sub = half // SUBS
    slots = ids_ref.shape[0]
    n_msg = n_dp * 16
    nx = 4
    dp, me = lax.axis_index("dp"), lax.axis_index("blk")
    right = (dp, lax.rem(me + 1, nx))
    left = (dp, lax.rem(me + nx - 1, nx))
    across = (dp, lax.rem(me + 2, nx))

    barrier = pltpu.get_barrier_semaphore()
    plane = jnp.where(me == HUB, AIDE, me)

    @pl.when(me != HUB)
    def _():
        pl.semaphore_signal(barrier, inc=1, device_id=(dp, HUB), device_id_type=MESH)

    def greet(j):
        peer = lax.rem(dp + j + 1, n_dp)
        pl.semaphore_signal(barrier, inc=1, device_id=(peer, plane), device_id_type=MESH)

    loop(n_dp - 1, greet)
    small_in = [
        pltpu.make_async_copy(src, dst, local_sem.at[3 + i])
        for i, (src, dst) in enumerate(((ids_hbm, ids_ref), (counts_hbm, counts_ref), (home_hbm, home_ref)))
    ]
    for copy in small_in:
        copy.start()
    q_in = pltpu.make_async_copy(q_hbm, qv.at[pl.ds(0, qd)], local_sem.at[0])
    p_in = pltpu.make_async_copy(p_hbm, pv, local_sem.at[1])
    t_in = pltpu.make_async_copy(t_hbm, tv, local_sem.at[2])
    q_in.start()
    p_in.start()
    t_in.start()

    @pl.when(me == HUB)
    def _():
        pl.semaphore_wait(barrier, nx - 1)
        for b in range(nx):
            if b != HUB:
                pl.semaphore_signal(group_there, inc=1, device_id=(dp, b), device_id_type=MESH)

    @pl.when(me != HUB)
    def _():
        pl.semaphore_wait(group_there, 1)


    def remote(src, dst, send, recv, peer):
        return pltpu.make_async_remote_copy(
            src_ref=src, dst_ref=dst, send_sem=send, recv_sem=recv, device_id=peer, device_id_type=MESH
        )

    def half_rows(block, part, k=0, n=half):
        return pl.ds(block * qd + part * half + k * sub, n)

    def gather_step(i, src, block, part, peer):
        return remote(src, qv.at[half_rows(block, part)], ag_s.at[i], ag_r.at[i], peer)

    own = [q_hbm.at[pl.ds(0, half)], q_hbm.at[pl.ds(half, half)]]
    ag_r1 = gather_step(0, own[0], 1, 0, right)
    ag_l1 = gather_step(1, own[1], 1, 1, left)
    ag_r2 = gather_step(2, own[1], 2, 1, right)
    ag_l2 = gather_step(3, own[0], 2, 0, left)
    ag_r3 = gather_step(4, qv.at[half_rows(1, 0)], 3, 0, right)
    ag_l3 = gather_step(5, qv.at[half_rows(1, 1)], 3, 1, left)
    for copy in (ag_r1, ag_l1, ag_r2, ag_l2):
        copy.start()

    for copy in small_in:
        copy.wait()
    ids, home = ids_ref[...], home_ref[...]
    book = jnp.concatenate([lax.shift_right_logical(home, 7), lax.bitwise_and(home, 127)], 1)
    book = book.astype(F32).T.astype(BF16)
    n_hi = home.shape[0]
    together = 4
    named_rows = []
    for k in range(0, slots, together):
        id_row = jnp.concatenate([ids[k + i : k + i + 1] for i in range(together)], 1)
        pick = one_hot(lax.shift_right_logical(id_row, 7) == iota((n_hi, together * qd), 0))
        found = nn(book, pick)
        found = found[:128] * 128.0 + found[128:]
        mine = lax.bitwise_and(id_row, 127) == iota((128, together * qd), 0)
        row = jnp.sum(jnp.where(mine, found, 0.0), 0, keepdims=True).astype(I32)
        named_rows += [row[:, i * qd : (i + 1) * qd] for i in range(together)]
    rows = jnp.zeros((slots, qd), I32)
    for k in range(slots):
        rows = jnp.where(iota((slots, qd), 0) == k, named_rows[k], rows)
    live = iota((slots, qd), 0) < counts_ref[...]
    place = lax.bitwise_and(rows, 1023)
    meta_hi = jnp.where(live, lax.shift_right_logical(place, 5), -1).astype(F32)
    meta_lo = lax.bitwise_and(place, 31).astype(F32)
    blank = jnp.zeros((META - slots, qd), F32)
    meta_hi = jnp.concatenate([meta_hi, blank], 0).astype(BF16)
    meta_lo = jnp.concatenate([meta_lo, blank], 0).astype(BF16)
    owner_row = lax.shift_right_logical(named_rows[0], 10)
    width = 512

    def fill(buf, mats, src):
        def body(t):
            at = pl.multiple_of(t * width, width)
            total = nn(mats[0], src[pl.ds(0, qd), pl.ds(at, width)])
            for c in range(1, PIECES):
                total += nn(mats[c], src[pl.ds(0, qd), pl.ds(pl.multiple_of(at + c * piece, width), width)])
            buf[:, pl.ds(at, width)] = total.astype(BF16)

        loop(piece // width, body)

    def deliver(out, inn, send, recv):
        def copy(j, frm):
            to = lax.rem(dp + j, n_dp)
            return remote(
                out.at[pl.ds(pl.multiple_of(to * 16, 16), 16)],
                inn.at[pl.ds(pl.multiple_of(frm * 16, 16), 16)],
                send.at[0], recv.at[0], (to, me),
            )

        every = pl.ds(0, (n_dp - 1) * 16)
        whole = remote(out.at[every], inn.at[every], send.at[0], recv.at[0], right)

        def begin():
            loop(n_dp - 1, lambda j: copy(j + 1, dp).start())
            mine = pl.ds(pl.multiple_of(dp * 16, 16), 16)
            inn[mine, :] = out[mine, :]

        def arrived():
            whole.wait_recv()

        def sent():
            whole.wait_send()

        return begin, arrived, sent

    request, request_in, request_sent = deliver(req_out, req_in, rq_s, rq_r)
    answer, answer_in, answer_sent = deliver(ret_out, ret_in, rt_s, rt_r)

    q_in.wait()
    pack = [message_rows(n_msg, owner_row, c) for c in range(PIECES)]
    fill(req_out, pack, qv)
    req_out[:, piece:] = (nt(pack[0], meta_hi) + nt(pack[1], meta_lo)).astype(BF16)

    def scores(block):
        cols = pl.ds(block * qd, qd)
        s_ref[:, cols] = SCALE * nt(pv[...], qv[cols, :])
        s = s_ref[:, cols]
        top = jnp.max(s, 0, keepdims=True)
        e = jnp.exp(s - top)
        stats[block, 0:1, :] = top
        stats[block, 1:2, :] = jnp.sum(e, 0, keepdims=True)
        for j in range(pd // 128):
            e_ref[:, j * 128 : (j + 1) * 128] = e[j * 128 : (j + 1) * 128].T.astype(BF16)

    wide = 2048

    def sums(dst, at):
        def body(t):
            cols = pl.ds(pl.multiple_of(t * wide, wide), wide)
            dst[pl.ds(at, qd), cols] = nn(e_ref[...], pv[:, cols]).astype(dst.dtype)

        loop(d // wide, body)

    p_in.wait()
    scores(0)
    sums(base, 0)
    @pl.when(me == AIDE)
    def _():
        pl.semaphore_wait(barrier, 2 * (n_dp - 1))
        pl.semaphore_signal(peers_there, inc=1, device_id=(dp, HUB), device_id_type=MESH)

    @pl.when((me != HUB) & (me != AIDE))
    def _():
        pl.semaphore_wait(barrier, n_dp - 1)

    @pl.when(me == HUB)
    def _():
        pl.semaphore_wait(peers_there, 1)

    request()

    ag_r1.wait_recv()
    ag_r3.start()
    ag_l1.wait_recv()
    ag_l3.start()
    scores(1)
    sums(ob, 0)

    ag_r2.wait_recv()
    ag_l2.wait_recv()
    scores(2)
    sums(ob, qd)

    def back_step(i, block, part, k, n, dst, at, peer):
        src = ob.at[half_rows(block - 1, part, k, n)]
        return remote(src, dst.at[pl.ds(at, n)], rs_s.at[i], rs_r.at[i], peer)

    b_r = [back_step(0, 1, 1, 0, half, grecv.at[0], half, right)]
    b_l = [back_step(1, 1, 0, 0, half, grecv.at[1], 0, left)]
    a_r = [back_step(2 + 4 * k, 3, 0, k, sub, arecv.at[0], k * sub, right) for k in range(SUBS)]
    a_l = [back_step(3 + 4 * k, 3, 1, k, sub, arecv.at[1], k * sub, left) for k in range(SUBS)]
    c_r = [back_step(4 + 4 * k, 2, 0, k, sub, grecv.at[0], k * sub, right) for k in range(SUBS)]
    c_l = [back_step(5 + 4 * k, 2, 1, k, sub, grecv.at[1], half + k * sub, left) for k in range(SUBS)]
    for copy in b_r + b_l:
        copy.start()
    request_in()
    t_in.wait()
    asker = lax.shift_right_logical(iota((qd, 1), 0), 2)
    for c in range(PIECES):
        qr[:, c * piece : (c + 1) * piece] = nn(query_rows(n_msg, asker, c), req_in[:, :piece]).astype(BF16)
    asker = lax.shift_right_logical(iota((1, qd), 1), 2)
    back = [message_rows(n_msg, asker, c) for c in range(PIECES)]
    tail = req_in[:, piece:]
    places = tn(tail, back[0]) * 32.0 + tn(tail, back[1])
    sneg[...] = SCALE * nt(tv[...], qr[...])
    n_rows = tv.shape[0]

    def neg_top(t, top):
        at = pl.ds(pl.multiple_of(t * 128, 128), 128)
        index = (iota((128, qd), 0) + t * 128).astype(F32)
        times = jnp.zeros((128, qd), F32)
        for k in range(slots):
            times += jnp.where(places[k : k + 1] == index, 1.0, 0.0)
        times_ref[at, :] = times
        return jnp.maximum(top, jnp.max(jnp.where(times > 0.0, sneg[at, :], -jnp.inf), 0, keepdims=True))

    m_far = lax.fori_loop(0, n_rows // 128, neg_top, jnp.full((1, qd), -jnp.inf, F32))

    def neg_weights(t, total):
        at = pl.ds(pl.multiple_of(t * 128, 128), 128)
        times = times_ref[at, :]
        e = jnp.where(times > 0.0, times * jnp.exp(jnp.minimum(sneg[at, :] - m_far, 0.0)), 0.0)
        eneg[:, at] = e.T.astype(BF16)
        return total + jnp.sum(e, 0, keepdims=True)

    l_far = lax.fori_loop(0, n_rows // 128, neg_weights, jnp.zeros((1, qd), F32))

    def neg_sums(t):
        cols = pl.ds(pl.multiple_of(t * wide, wide), wide)
        oneg[:, cols] = nn(eneg[...], tv[:, cols]).astype(BF16)

    loop(d // wide, neg_sums)
    fill(ret_out, back, oneg)
    line = iota((META, qd), 0)
    rest = jnp.where(line == 0, m_far, jnp.where(line == 1, l_far, 0.0))
    tail = jnp.zeros((n_msg, META), F32)
    for c in range(3):
        part = rest.astype(BF16)
        rest = rest - part.astype(F32)
        tail += nt(back[c], part)
    ret_out[:, piece:] = tail.astype(BF16)
    answer()

    ag_r3.wait_recv()
    ag_l3.wait_recv()
    scores(3)

    first = iota((8, qd), 1) < half
    picks = [stats[block, :, :] for block in range(nx)]
    st_out[0, :, :] = jnp.where(first, picks[2], picks[1])
    st_out[1, :, :] = picks[3]
    st_out[2, :, :] = jnp.where(first, picks[1], picks[2])
    st_out[3, :, :] = picks[3]
    st_right = remote(st_out.at[pl.ds(0, 2)], st_in.at[pl.ds(0, 2)], st_s.at[0], st_r.at[0], right)
    st_left = remote(st_out.at[pl.ds(2, 2)], st_in.at[pl.ds(2, 2)], st_s.at[1], st_r.at[1], left)
    st_across = remote(st_out.at[pl.ds(1, 1)], st_in.at[pl.ds(4, 1)], st_s.at[2], st_r.at[2], across)
    st_copies = [st_right, st_left, st_across]
    for copy in st_copies:
        copy.start()
    sums(ob, 2 * qd)
    for k in range(SUBS):
        a_r[k].start()
        a_l[k].start()

    answer_in()
    tail = ret_in[:, piece:]
    neg_stats = tn(tail, pack[0]) + tn(tail, pack[1]) + tn(tail, pack[2])
    for copy in st_copies:
        copy.wait_recv()

    def stat(entry, i):
        return st_in[entry, i : i + 1, :]

    m_own, l_own = stats[0, 0:1, :], stats[0, 1:2, :]
    m_l, l_l, m_r, l_r, m_x, l_x = (stat(e, i) for e in (0, 2, 4) for i in (0, 1))
    m_n, l_n = neg_stats[0:1], neg_stats[1:2]
    pairs = ((m_own, l_own), (m_l, l_l), (m_r, l_r), (m_x, l_x), (m_n, l_n))
    top = functools.reduce(jnp.maximum, [m for m, _ in pairs])
    lse = top + jnp.log(sum(l * jnp.exp(m - top) for m, l in pairs))
    lse_out[...] = jnp.broadcast_to(lse, (8, qd))
    lse_copies = [
        remote(lse_out, lse_in.at[i], ls_s.at[i], ls_r.at[i], peer)
        for i, peer in enumerate((right, left, across))
    ]
    for copy in lse_copies:
        copy.start()
    eye = iota((qd, qd), 0) == iota((qd, qd), 1)
    loss_ref[...] = lse - jnp.sum(jnp.where(eye, s_ref[pl.ds(0, qd), pl.ds(0, qd)], 0.0), 0, keepdims=True)

    f_own, f_n = to_col(jnp.exp(m_own - lse)), to_col(jnp.exp(m_n - lse))
    owner_col = to_col(owner_row)
    for c in range(PIECES):
        cols = pl.ds(c * piece, piece)
        neg = nn(query_rows(n_msg, owner_col, c), ret_in[:, :piece])
        base[:, cols] = f_own * base[:, cols] + f_n * neg - pv[pl.ds(0, qd), cols].astype(F32)

    front = iota((1, qd), 1) < half

    m_near = stats[2, 0:1, :]
    m_away = jnp.where(front, stat(1, 0), stat(3, 0))
    m_both = jnp.maximum(m_near, m_away)
    factors[0, :, :] = jnp.broadcast_to(to_col(jnp.exp(m_near - m_both)), (qd, 128))
    factors[1, :, :] = jnp.broadcast_to(to_col(jnp.exp(m_away - m_both)), (qd, 128))

    def merge(part, k):
        at, far_at = part * half + k * sub, pl.ds(k * sub, sub)
        f_near, f_away = factors[0, pl.ds(at, sub), :1], factors[1, pl.ds(at, sub), :1]

        def body(t):
            cols = pl.ds(pl.multiple_of(t * 1024, 1024), 1024)
            here = ob[pl.ds(qd + at, sub), cols].astype(F32)
            total = f_near * here + f_away * arecv[part, far_at, cols].astype(F32)
            ob[pl.ds(qd + at, sub), cols] = total.astype(BF16)

        loop(d // 1024, body)

    for k in range(SUBS):
        a_r[k].wait_recv()
        merge(0, k)
        c_r[k].start()
        a_l[k].wait_recv()
        merge(1, k)
        c_l[k].start()

    for copy in lse_copies:
        copy.wait_recv()
    lse_l, lse_r, lse_x = (lse_in[i, 0:1, :] for i in range(3))
    by_block = (lse, jnp.where(front, lse_l, lse_r), jnp.where(front, lse_r, lse_l), lse_x)
    for block in range(nx):
        cols = pl.ds(block * qd, qd)
        wt_ref[:, cols] = jnp.exp(s_ref[:, cols] - by_block[block]).astype(BF16)
    span = 1024

    def passage_grads(t):
        cols = pl.ds(pl.multiple_of(t * span, span), span)
        total = nn(wt_ref[...], qv[:, cols])
        gp_ref[pl.ds(qd, pd - qd), cols] = (SCALE * total[qd:]).astype(BF16)
        gp_ref[pl.ds(0, qd), cols] = (SCALE * (total[:qd] - qv[pl.ds(0, qd), cols].astype(F32))).astype(BF16)

    loop(d // span, passage_grads)

    request_sent()
    answer_sent()

    top_l, top_r = jnp.maximum(m_l, m_x), jnp.maximum(m_r, m_x)
    factors[2, :, :] = jnp.broadcast_to(to_col(jnp.exp(jnp.where(front, top_l, m_l) - lse)), (qd, 128))
    factors[3, :, :] = jnp.broadcast_to(to_col(jnp.exp(jnp.where(front, m_r, top_r) - lse)), (qd, 128))

    def finish(at):
        f_l, f_r = factors[2, pl.ds(at, sub), :1], factors[3, pl.ds(at, sub), :1]

        def body(t):
            cols = pl.ds(pl.multiple_of(t * 1024, 1024), 1024)
            total = base[pl.ds(at, sub), cols]
            total += f_l * grecv[0, pl.ds(at, sub), cols].astype(F32)
            total += f_r * grecv[1, pl.ds(at, sub), cols].astype(F32)
            gq_ref[pl.ds(at, sub), cols] = (SCALE * total).astype(BF16)

        loop(d // 1024, body)

    for copy in b_r + b_l:
        copy.wait_recv()
    for k in range(SUBS):
        c_r[k].wait_recv()
        finish(k * sub)
        c_l[k].wait_recv()
        finish(half + k * sub)

    for copy in [ag_r1, ag_r2, ag_r3, ag_l1, ag_l2, ag_l3] + b_r + b_l + a_r + a_l + c_r + c_l + st_copies + lse_copies:
        copy.wait_send()


def write_kernel(gp_in, gq_in, loss_in, gp_out, gq_out, loss_out, sems):
    parts = 4
    n = gp_in.shape[0] // parts
    copies = [
        pltpu.make_async_copy(gp_in.at[pl.ds(i * n, n)], gp_out.at[pl.ds(i * n, n)], sems.at[i]) for i in range(parts)
    ]
    copies.append(pltpu.make_async_copy(gq_in, gq_out, sems.at[parts]))
    copies.append(pltpu.make_async_copy(loss_in, loss_out, sems.at[parts + 1]))
    for copy in copies:
        copy.start()
    for copy in copies:
        copy.wait()


def per_device(n_dp, queries, passages, neg_table, neg_ids, counts, neg_home):
    qd, d = queries.shape
    pd = passages.shape[0]
    n_rows = neg_table.shape[0]
    nx, half = 4, qd // 2
    n_msg, piece = n_dp * 16, d // PIECES
    any_spec = pl.BlockSpec(memory_space=pl.ANY)
    vmem_spec = pl.BlockSpec(memory_space=pltpu.VMEM)
    dma = pltpu.SemaphoreType.DMA
    grad_p, grad_q, loss = pl.pallas_call(
        functools.partial(exchange_kernel, n_dp),
        out_shape=(
            pltpu.VMEM((pd, d), BF16),
            pltpu.VMEM((qd, d), BF16),
            pltpu.VMEM((1, qd), F32),
        ),
        in_specs=[any_spec] * 6,
        out_specs=(vmem_spec, vmem_spec, vmem_spec),
        scratch_shapes=[
            pltpu.VMEM(neg_ids.T.shape, I32),
            pltpu.VMEM((1, qd), I32),
            pltpu.VMEM((neg_home.shape[0] // 128, 128), I32),
            pltpu.VMEM((nx * qd, d), BF16),
            pltpu.VMEM((pd, d), BF16),
            pltpu.VMEM((n_rows, d), BF16),
            pltpu.VMEM((pd, nx * qd), F32),
            pltpu.VMEM((qd, pd), BF16),
            pltpu.VMEM((pd, nx * qd), BF16),
            pltpu.VMEM((nx, 8, qd), F32),
            pltpu.VMEM(((nx - 1) * qd, d), BF16),
            pltpu.VMEM((qd, d), F32),
            pltpu.VMEM((2, half, d), BF16),
            pltpu.VMEM((2, qd, d), BF16),
            pltpu.VMEM((n_msg, piece + META), BF16),
            pltpu.VMEM((n_msg, piece + META), BF16),
            pltpu.VMEM((n_msg, piece + META), BF16),
            pltpu.VMEM((n_msg, piece + META), BF16),
            pltpu.VMEM((qd, d), BF16),
            pltpu.VMEM((n_rows, qd), F32),
            pltpu.VMEM((n_rows, qd), F32),
            pltpu.VMEM((qd, n_rows), BF16),
            pltpu.VMEM((qd, d), BF16),
            pltpu.VMEM((4, qd, 128), F32),
            pltpu.VMEM((4, 8, qd), F32),
            pltpu.VMEM((5, 8, qd), F32),
            pltpu.VMEM((8, qd), F32),
            pltpu.VMEM((3, 8, qd), F32),
            dma((6,)),
            dma((6,)),
            dma((6,)),
            dma((2 + 4 * SUBS,)),
            dma((2 + 4 * SUBS,)),
            dma((3,)),
            dma((3,)),
            dma((3,)),
            dma((3,)),
            dma((1,)),
            dma((1,)),
            dma((1,)),
            dma((1,)),
            pltpu.SemaphoreType.REGULAR,
            pltpu.SemaphoreType.REGULAR,
        ],
        compiler_params=pltpu.CompilerParams(
            collective_id=0, has_side_effects=True, vmem_limit_bytes=54 * 1024 * 1024
        ),
        cost_estimate=pl.CostEstimate(flops=13_000_000_000, bytes_accessed=25_000_000, transcendentals=1_000_000),
        name="exchange",
    )(queries, passages, neg_table, neg_ids.T, counts.reshape(1, qd), neg_home.reshape(-1, 128))
    grad_p, grad_q, loss = pl.pallas_call(
        write_kernel,
        out_shape=(
            jax.ShapeDtypeStruct((pd, d), BF16),
            jax.ShapeDtypeStruct((qd, d), BF16),
            jax.ShapeDtypeStruct((1, qd), F32),
        ),
        in_specs=[any_spec] * 3,
        out_specs=(any_spec, any_spec, any_spec),
        scratch_shapes=[dma((6,))],
        compiler_params=pltpu.CompilerParams(vmem_limit_bytes=1024 * 1024),
        cost_estimate=pl.CostEstimate(flops=0, bytes_accessed=7_300_000, transcendentals=0),
        name="write",
    )(grad_p, grad_q, loss)
    return loss.reshape(qd), grad_q, grad_p


def solution(mesh):
    in_specs = (
        P(("dp", "blk"), None),
        P(("dp", "blk"), None),
        P("dp", None),
        P(("dp", "blk"), None),
        P(("dp", "blk")),
        P(),
    )
    out_specs = (P(("dp", "blk")), P(("dp", "blk"), None), P(("dp", "blk"), None))
    return jax.shard_map(
        functools.partial(per_device, mesh.shape["dp"]),
        mesh=mesh, in_specs=in_specs, out_specs=out_specs, check_vma=False,
    )
```

```python
import functools

import jax
import jax.numpy as jnp
from jax import lax
from jax.experimental import pallas as pl
from jax.experimental.pallas import tpu as pltpu
from jax.sharding import PartitionSpec as P

MESH = pl.DeviceIdType.MESH
F32, BF16, I32 = jnp.float32, jnp.bfloat16, jnp.int32
SCALE = 0.0625
META = 128
PIECES = 4
SUBS = 2
HUB, AIDE = 2, 1


def nn(a, b):
    return jnp.dot(a, b, preferred_element_type=F32)


def nt(a, b):
    return lax.dot_general(a, b, (((1,), (1,)), ((), ())), preferred_element_type=F32)


def tn(a, b):
    return lax.dot_general(a, b, (((0,), (0,)), ((), ())), preferred_element_type=F32)


def iota(shape, dim):
    return lax.broadcasted_iota(I32, shape, dim)


def to_row(col):
    n = col.shape[0]
    eye = iota((n, n), 0) == iota((n, n), 1)
    return jnp.sum(jnp.where(eye, col, jnp.zeros_like(col)), 0, keepdims=True)


def to_col(row):
    n = row.shape[1]
    eye = iota((n, n), 0) == iota((n, n), 1)
    return jnp.sum(jnp.where(eye, row, jnp.zeros_like(row)), 1, keepdims=True)


def one_hot(cond):
    return jnp.where(cond, 1.0, 0.0).astype(BF16)


def loop(n, body):
    lax.fori_loop(0, n, lambda t, carry: (body(t), carry)[1], 0)


def message_rows(n_msg, who, c):
    t, i = iota((n_msg, who.shape[1]), 0), iota((n_msg, who.shape[1]), 1)
    return one_hot(
        (lax.shift_right_logical(t, 4) == who)
        & (lax.bitwise_and(lax.shift_right_logical(t, 2), 3) == c)
        & (lax.bitwise_and(t, 3) == lax.bitwise_and(i, 3))
    )


def query_rows(n_msg, who, c):
    i, t = iota((who.shape[0], n_msg), 0), iota((who.shape[0], n_msg), 1)
    return one_hot(
        (lax.shift_right_logical(t, 4) == who)
        & (lax.bitwise_and(lax.shift_right_logical(t, 2), 3) == c)
        & (lax.bitwise_and(t, 3) == lax.bitwise_and(i, 3))
    )


def exchange_kernel(
    n_dp, q_hbm, p_hbm, t_hbm, ids_hbm, counts_hbm, home_hbm,
    gp_ref, gq_ref, loss_ref,
    ids_ref, counts_ref, home_ref, qv, pv, tv, s_ref, e_ref, wt_ref, stats, ob, base, arecv, grecv,
    req_out, req_in, ret_out, ret_in, qr, sneg, times_ref, eneg, oneg, factors,
    st_out, st_in, lse_out, lse_in,
    local_sem, ag_s, ag_r, rs_s, rs_r, st_s, st_r, ls_s, ls_r,
    rq_s, rq_r, rt_s, rt_r, group_there, peers_there,
):
    qd, d = q_hbm.shape
    pd = p_hbm.shape[0]
    half, piece = qd // 2, d // PIECES
    sub = half // SUBS
    slots = ids_ref.shape[0]
    n_msg = n_dp * 16
    nx = 4
    dp, me = lax.axis_index("dp"), lax.axis_index("blk")
    right = (dp, lax.rem(me + 1, nx))
    left = (dp, lax.rem(me + nx - 1, nx))
    across = (dp, lax.rem(me + 2, nx))

    barrier = pltpu.get_barrier_semaphore()
    plane = jnp.where(me == HUB, AIDE, me)

    @pl.when(me != HUB)
    def _():
        pl.semaphore_signal(barrier, inc=1, device_id=(dp, HUB), device_id_type=MESH)

    def greet(j):
        peer = lax.rem(dp + j + 1, n_dp)
        pl.semaphore_signal(barrier, inc=1, device_id=(peer, plane), device_id_type=MESH)

    loop(n_dp - 1, greet)
    small_in = [
        pltpu.make_async_copy(src, dst, local_sem.at[3 + i])
        for i, (src, dst) in enumerate(((ids_hbm, ids_ref), (counts_hbm, counts_ref), (home_hbm, home_ref)))
    ]
    for copy in small_in:
        copy.start()
    q_in = pltpu.make_async_copy(q_hbm, qv.at[pl.ds(0, qd)], local_sem.at[0])
    p_in = pltpu.make_async_copy(p_hbm, pv, local_sem.at[1])
    t_in = pltpu.make_async_copy(t_hbm, tv, local_sem.at[2])
    q_in.start()
    p_in.start()
    t_in.start()

    @pl.when(me == HUB)
    def _():
        pl.semaphore_wait(barrier, nx - 1)
        for b in range(nx):
            if b != HUB:
                pl.semaphore_signal(group_there, inc=1, device_id=(dp, b), device_id_type=MESH)

    @pl.when(me != HUB)
    def _():
        pl.semaphore_wait(group_there, 1)


    def remote(src, dst, send, recv, peer):
        return pltpu.make_async_remote_copy(
            src_ref=src, dst_ref=dst, send_sem=send, recv_sem=recv, device_id=peer, device_id_type=MESH
        )

    def half_rows(block, part, k=0, n=half):
        return pl.ds(block * qd + part * half + k * sub, n)

    def gather_step(i, src, block, part, peer):
        return remote(src, qv.at[half_rows(block, part)], ag_s.at[i], ag_r.at[i], peer)

    own = [q_hbm.at[pl.ds(0, half)], q_hbm.at[pl.ds(half, half)]]
    ag_r1 = gather_step(0, own[0], 1, 0, right)
    ag_l1 = gather_step(1, own[1], 1, 1, left)
    ag_r2 = gather_step(2, own[1], 2, 1, right)
    ag_l2 = gather_step(3, own[0], 2, 0, left)
    ag_r3 = gather_step(4, qv.at[half_rows(1, 0)], 3, 0, right)
    ag_l3 = gather_step(5, qv.at[half_rows(1, 1)], 3, 1, left)
    for copy in (ag_r1, ag_l1, ag_r2, ag_l2):
        copy.start()

    for copy in small_in:
        copy.wait()
    ids, home = ids_ref[...], home_ref[...]
    book = jnp.concatenate([lax.shift_right_logical(home, 7), lax.bitwise_and(home, 127)], 1)
    book = book.astype(F32).T.astype(BF16)
    n_hi = home.shape[0]
    together = 4
    named_rows = []
    for k in range(0, slots, together):
        id_row = jnp.concatenate([ids[k + i : k + i + 1] for i in range(together)], 1)
        pick = one_hot(lax.shift_right_logical(id_row, 7) == iota((n_hi, together * qd), 0))
        found = nn(book, pick)
        found = found[:128] * 128.0 + found[128:]
        mine = lax.bitwise_and(id_row, 127) == iota((128, together * qd), 0)
        row = jnp.sum(jnp.where(mine, found, 0.0), 0, keepdims=True).astype(I32)
        named_rows += [row[:, i * qd : (i + 1) * qd] for i in range(together)]
    rows = jnp.zeros((slots, qd), I32)
    for k in range(slots):
        rows = jnp.where(iota((slots, qd), 0) == k, named_rows[k], rows)
    live = iota((slots, qd), 0) < counts_ref[...]
    place = lax.bitwise_and(rows, 1023)
    meta_hi = jnp.where(live, lax.shift_right_logical(place, 5), -1).astype(F32)
    meta_lo = lax.bitwise_and(place, 31).astype(F32)
    blank = jnp.zeros((META - slots, qd), F32)
    meta_hi = jnp.concatenate([meta_hi, blank], 0).astype(BF16)
    meta_lo = jnp.concatenate([meta_lo, blank], 0).astype(BF16)
    owner_row = lax.shift_right_logical(named_rows[0], 10)
    width = 512

    def fill(buf, mats, src):
        def body(t):
            at = pl.multiple_of(t * width, width)
            total = nn(mats[0], src[pl.ds(0, qd), pl.ds(at, width)])
            for c in range(1, PIECES):
                total += nn(mats[c], src[pl.ds(0, qd), pl.ds(pl.multiple_of(at + c * piece, width), width)])
            buf[:, pl.ds(at, width)] = total.astype(BF16)

        loop(piece // width, body)

    def deliver(out, inn, send, recv):
        def copy(j, frm):
            to = lax.rem(dp + j, n_dp)
            return remote(
                out.at[pl.ds(pl.multiple_of(to * 16, 16), 16)],
                inn.at[pl.ds(pl.multiple_of(frm * 16, 16), 16)],
                send.at[0], recv.at[0], (to, me),
            )

        every = pl.ds(0, (n_dp - 1) * 16)
        whole = remote(out.at[every], inn.at[every], send.at[0], recv.at[0], right)

        def begin():
            loop(n_dp - 1, lambda j: copy(j + 1, dp).start())
            mine = pl.ds(pl.multiple_of(dp * 16, 16), 16)
            inn[mine, :] = out[mine, :]

        def arrived():
            whole.wait_recv()

        def sent():
            whole.wait_send()

        return begin, arrived, sent

    request, request_in, request_sent = deliver(req_out, req_in, rq_s, rq_r)
    answer, answer_in, answer_sent = deliver(ret_out, ret_in, rt_s, rt_r)

    q_in.wait()
    pack = [message_rows(n_msg, owner_row, c) for c in range(PIECES)]
    fill(req_out, pack, qv)
    req_out[:, piece:] = (nt(pack[0], meta_hi) + nt(pack[1], meta_lo)).astype(BF16)

    def scores(block):
        cols = pl.ds(block * qd, qd)
        s_ref[:, cols] = SCALE * nt(pv[...], qv[cols, :])
        s = s_ref[:, cols]
        top = jnp.max(s, 0, keepdims=True)
        e = jnp.exp(s - top)
        stats[block, 0:1, :] = top
        stats[block, 1:2, :] = jnp.sum(e, 0, keepdims=True)
        for j in range(pd // 128):
            e_ref[:, j * 128 : (j + 1) * 128] = e[j * 128 : (j + 1) * 128].T.astype(BF16)

    wide = 2048

    def sums(dst, at):
        def body(t):
            cols = pl.ds(pl.multiple_of(t * wide, wide), wide)
            dst[pl.ds(at, qd), cols] = nn(e_ref[...], pv[:, cols]).astype(dst.dtype)

        loop(d // wide, body)

    p_in.wait()
    scores(0)
    sums(base, 0)
    @pl.when(me == AIDE)
    def _():
        pl.semaphore_wait(barrier, 2 * (n_dp - 1))
        pl.semaphore_signal(peers_there, inc=1, device_id=(dp, HUB), device_id_type=MESH)

    @pl.when((me != HUB) & (me != AIDE))
    def _():
        pl.semaphore_wait(barrier, n_dp - 1)

    @pl.when(me == HUB)
    def _():
        pl.semaphore_wait(peers_there, 1)

    request()

    ag_r1.wait_recv()
    ag_r3.start()
    ag_l1.wait_recv()
    ag_l3.start()
    scores(1)
    sums(ob, 0)

    ag_r2.wait_recv()
    ag_l2.wait_recv()
    scores(2)
    sums(ob, qd)

    def back_step(i, block, part, k, n, dst, at, peer):
        src = ob.at[half_rows(block - 1, part, k, n)]
        return remote(src, dst.at[pl.ds(at, n)], rs_s.at[i], rs_r.at[i], peer)

    b_r = [back_step(0, 1, 1, 0, half, grecv.at[0], half, right)]
    b_l = [back_step(1, 1, 0, 0, half, grecv.at[1], 0, left)]
    a_r = [back_step(2 + 4 * k, 3, 0, k, sub, arecv.at[0], k * sub, right) for k in range(SUBS)]
    a_l = [back_step(3 + 4 * k, 3, 1, k, sub, arecv.at[1], k * sub, left) for k in range(SUBS)]
    c_r = [back_step(4 + 4 * k, 2, 0, k, sub, grecv.at[0], k * sub, right) for k in range(SUBS)]
    c_l = [back_step(5 + 4 * k, 2, 1, k, sub, grecv.at[1], half + k * sub, left) for k in range(SUBS)]
    for copy in b_r + b_l:
        copy.start()
    request_in()
    t_in.wait()
    asker = lax.shift_right_logical(iota((qd, 1), 0), 2)
    for c in range(PIECES):
        qr[:, c * piece : (c + 1) * piece] = nn(query_rows(n_msg, asker, c), req_in[:, :piece]).astype(BF16)
    asker = lax.shift_right_logical(iota((1, qd), 1), 2)
    back = [message_rows(n_msg, asker, c) for c in range(PIECES)]
    tail = req_in[:, piece:]
    places = tn(tail, back[0]) * 32.0 + tn(tail, back[1])
    sneg[...] = SCALE * nt(tv[...], qr[...])
    n_rows = tv.shape[0]

    def neg_top(t, top):
        at = pl.ds(pl.multiple_of(t * 128, 128), 128)
        index = (iota((128, qd), 0) + t * 128).astype(F32)
        times = jnp.zeros((128, qd), F32)
        for k in range(slots):
            times += jnp.where(places[k : k + 1] == index, 1.0, 0.0)
        times_ref[at, :] = times
        return jnp.maximum(top, jnp.max(jnp.where(times > 0.0, sneg[at, :], -jnp.inf), 0, keepdims=True))

    m_far = lax.fori_loop(0, n_rows // 128, neg_top, jnp.full((1, qd), -jnp.inf, F32))

    def neg_weights(t, total):
        at = pl.ds(pl.multiple_of(t * 128, 128), 128)
        times = times_ref[at, :]
        e = jnp.where(times > 0.0, times * jnp.exp(jnp.minimum(sneg[at, :] - m_far, 0.0)), 0.0)
        eneg[:, at] = e.T.astype(BF16)
        return total + jnp.sum(e, 0, keepdims=True)

    l_far = lax.fori_loop(0, n_rows // 128, neg_weights, jnp.zeros((1, qd), F32))

    def neg_sums(t):
        cols = pl.ds(pl.multiple_of(t * wide, wide), wide)
        oneg[:, cols] = nn(eneg[...], tv[:, cols]).astype(BF16)

    loop(d // wide, neg_sums)
    fill(ret_out, back, oneg)
    line = iota((META, qd), 0)
    rest = jnp.where(line == 0, m_far, jnp.where(line == 1, l_far, 0.0))
    tail = jnp.zeros((n_msg, META), F32)
    for c in range(3):
        part = rest.astype(BF16)
        rest = rest - part.astype(F32)
        tail += nt(back[c], part)
    ret_out[:, piece:] = tail.astype(BF16)
    answer()

    ag_r3.wait_recv()
    ag_l3.wait_recv()
    scores(3)

    first = iota((8, qd), 1) < half
    picks = [stats[block, :, :] for block in range(nx)]
    st_out[0, :, :] = jnp.where(first, picks[2], picks[1])
    st_out[1, :, :] = picks[3]
    st_out[2, :, :] = jnp.where(first, picks[1], picks[2])
    st_out[3, :, :] = picks[3]
    st_right = remote(st_out.at[pl.ds(0, 2)], st_in.at[pl.ds(0, 2)], st_s.at[0], st_r.at[0], right)
    st_left = remote(st_out.at[pl.ds(2, 2)], st_in.at[pl.ds(2, 2)], st_s.at[1], st_r.at[1], left)
    st_across = remote(st_out.at[pl.ds(1, 1)], st_in.at[pl.ds(4, 1)], st_s.at[2], st_r.at[2], across)
    st_copies = [st_right, st_left, st_across]
    for copy in st_copies:
        copy.start()
    sums(ob, 2 * qd)
    for k in range(SUBS):
        a_r[k].start()
        a_l[k].start()

    answer_in()
    tail = ret_in[:, piece:]
    neg_stats = tn(tail, pack[0]) + tn(tail, pack[1]) + tn(tail, pack[2])
    for copy in st_copies:
        copy.wait_recv()

    def stat(entry, i):
        return st_in[entry, i : i + 1, :]

    m_own, l_own = stats[0, 0:1, :], stats[0, 1:2, :]
    m_l, l_l, m_r, l_r, m_x, l_x = (stat(e, i) for e in (0, 2, 4) for i in (0, 1))
    m_n, l_n = neg_stats[0:1], neg_stats[1:2]
    pairs = ((m_own, l_own), (m_l, l_l), (m_r, l_r), (m_x, l_x), (m_n, l_n))
    top = functools.reduce(jnp.maximum, [m for m, _ in pairs])
    lse = top + jnp.log(sum(l * jnp.exp(m - top) for m, l in pairs))
    lse_out[...] = jnp.broadcast_to(lse, (8, qd))
    lse_copies = [
        remote(lse_out, lse_in.at[i], ls_s.at[i], ls_r.at[i], peer)
        for i, peer in enumerate((right, left, across))
    ]
    for copy in lse_copies:
        copy.start()
    eye = iota((qd, qd), 0) == iota((qd, qd), 1)
    loss_ref[...] = lse - jnp.sum(jnp.where(eye, s_ref[pl.ds(0, qd), pl.ds(0, qd)], 0.0), 0, keepdims=True)

    f_own, f_n = to_col(jnp.exp(m_own - lse)), to_col(jnp.exp(m_n - lse))
    owner_col = to_col(owner_row)
    for c in range(PIECES):
        cols = pl.ds(c * piece, piece)
        neg = nn(query_rows(n_msg, owner_col, c), ret_in[:, :piece])
        base[:, cols] = f_own * base[:, cols] + f_n * neg - pv[pl.ds(0, qd), cols].astype(F32)

    front = iota((1, qd), 1) < half

    m_near = stats[2, 0:1, :]
    m_away = jnp.where(front, stat(1, 0), stat(3, 0))
    m_both = jnp.maximum(m_near, m_away)
    factors[0, :, :] = jnp.broadcast_to(to_col(jnp.exp(m_near - m_both)), (qd, 128))
    factors[1, :, :] = jnp.broadcast_to(to_col(jnp.exp(m_away - m_both)), (qd, 128))

    def merge(part, k):
        at, far_at = part * half + k * sub, pl.ds(k * sub, sub)
        f_near, f_away = factors[0, pl.ds(at, sub), :1], factors[1, pl.ds(at, sub), :1]

        def body(t):
            cols = pl.ds(pl.multiple_of(t * 1024, 1024), 1024)
            here = ob[pl.ds(qd + at, sub), cols].astype(F32)
            total = f_near * here + f_away * arecv[part, far_at, cols].astype(F32)
            ob[pl.ds(qd + at, sub), cols] = total.astype(BF16)

        loop(d // 1024, body)

    for k in range(SUBS):
        a_r[k].wait_recv()
        merge(0, k)
        c_r[k].start()
        a_l[k].wait_recv()
        merge(1, k)
        c_l[k].start()

    for copy in lse_copies:
        copy.wait_recv()
    lse_l, lse_r, lse_x = (lse_in[i, 0:1, :] for i in range(3))
    by_block = (lse, jnp.where(front, lse_l, lse_r), jnp.where(front, lse_r, lse_l), lse_x)
    for block in range(nx):
        cols = pl.ds(block * qd, qd)
        wt_ref[:, cols] = jnp.exp(s_ref[:, cols] - by_block[block]).astype(BF16)
    span = 1024

    def passage_grads(t):
        cols = pl.ds(pl.multiple_of(t * span, span), span)
        total = nn(wt_ref[...], qv[:, cols])
        gp_ref[pl.ds(qd, pd - qd), cols] = (SCALE * total[qd:]).astype(BF16)
        gp_ref[pl.ds(0, qd), cols] = (SCALE * (total[:qd] - qv[pl.ds(0, qd), cols].astype(F32))).astype(BF16)

    loop(d // span, passage_grads)

    request_sent()
    answer_sent()

    top_l, top_r = jnp.maximum(m_l, m_x), jnp.maximum(m_r, m_x)
    factors[2, :, :] = jnp.broadcast_to(to_col(jnp.exp(jnp.where(front, top_l, m_l) - lse)), (qd, 128))
    factors[3, :, :] = jnp.broadcast_to(to_col(jnp.exp(jnp.where(front, m_r, top_r) - lse)), (qd, 128))

    def finish(at):
        f_l, f_r = factors[2, pl.ds(at, sub), :1], factors[3, pl.ds(at, sub), :1]

        def body(t):
            cols = pl.ds(pl.multiple_of(t * 2048, 2048), 2048)
            total = base[pl.ds(at, sub), cols]
            total += f_l * grecv[0, pl.ds(at, sub), cols].astype(F32)
            total += f_r * grecv[1, pl.ds(at, sub), cols].astype(F32)
            gq_ref[pl.ds(at, sub), cols] = (SCALE * total).astype(BF16)

        loop(d // 2048, body)

    for copy in b_r + b_l:
        copy.wait_recv()
    for copy in [ag_r1, ag_r2, ag_r3, ag_l1, ag_l2, ag_l3] + b_r + b_l + a_r + a_l + st_copies + lse_copies:
        copy.wait_send()
    for k in range(SUBS):
        c_r[k].wait_recv()
        finish(k * sub)
        c_l[k].wait_recv()
        finish(half + k * sub)

    for copy in c_r + c_l:
        copy.wait_send()


def write_kernel(gp_in, gq_in, loss_in, gp_out, gq_out, loss_out, sems):
    parts = 4
    n = gp_in.shape[0] // parts
    copies = [
        pltpu.make_async_copy(gp_in.at[pl.ds(i * n, n)], gp_out.at[pl.ds(i * n, n)], sems.at[i]) for i in range(parts)
    ]
    copies.append(pltpu.make_async_copy(gq_in, gq_out, sems.at[parts]))
    copies.append(pltpu.make_async_copy(loss_in, loss_out, sems.at[parts + 1]))
    for copy in copies:
        copy.start()
    for copy in copies:
        copy.wait()


def per_device(n_dp, queries, passages, neg_table, neg_ids, counts, neg_home):
    qd, d = queries.shape
    pd = passages.shape[0]
    n_rows = neg_table.shape[0]
    nx, half = 4, qd // 2
    n_msg, piece = n_dp * 16, d // PIECES
    any_spec = pl.BlockSpec(memory_space=pl.ANY)
    vmem_spec = pl.BlockSpec(memory_space=pltpu.VMEM)
    dma = pltpu.SemaphoreType.DMA
    grad_p, grad_q, loss = pl.pallas_call(
        functools.partial(exchange_kernel, n_dp),
        out_shape=(
            pltpu.VMEM((pd, d), BF16),
            pltpu.VMEM((qd, d), BF16),
            pltpu.VMEM((1, qd), F32),
        ),
        in_specs=[any_spec] * 6,
        out_specs=(vmem_spec, vmem_spec, vmem_spec),
        scratch_shapes=[
            pltpu.VMEM(neg_ids.T.shape, I32),
            pltpu.VMEM((1, qd), I32),
            pltpu.VMEM((neg_home.shape[0] // 128, 128), I32),
            pltpu.VMEM((nx * qd, d), BF16),
            pltpu.VMEM((pd, d), BF16),
            pltpu.VMEM((n_rows, d), BF16),
            pltpu.VMEM((pd, nx * qd), F32),
            pltpu.VMEM((qd, pd), BF16),
            pltpu.VMEM((pd, nx * qd), BF16),
            pltpu.VMEM((nx, 8, qd), F32),
            pltpu.VMEM(((nx - 1) * qd, d), BF16),
            pltpu.VMEM((qd, d), F32),
            pltpu.VMEM((2, half, d), BF16),
            pltpu.VMEM((2, qd, d), BF16),
            pltpu.VMEM((n_msg, piece + META), BF16),
            pltpu.VMEM((n_msg, piece + META), BF16),
            pltpu.VMEM((n_msg, piece + META), BF16),
            pltpu.VMEM((n_msg, piece + META), BF16),
            pltpu.VMEM((qd, d), BF16),
            pltpu.VMEM((n_rows, qd), F32),
            pltpu.VMEM((n_rows, qd), F32),
            pltpu.VMEM((qd, n_rows), BF16),
            pltpu.VMEM((qd, d), BF16),
            pltpu.VMEM((4, qd, 128), F32),
            pltpu.VMEM((4, 8, qd), F32),
            pltpu.VMEM((5, 8, qd), F32),
            pltpu.VMEM((8, qd), F32),
            pltpu.VMEM((3, 8, qd), F32),
            dma((6,)),
            dma((6,)),
            dma((6,)),
            dma((2 + 4 * SUBS,)),
            dma((2 + 4 * SUBS,)),
            dma((3,)),
            dma((3,)),
            dma((3,)),
            dma((3,)),
            dma((1,)),
            dma((1,)),
            dma((1,)),
            dma((1,)),
            pltpu.SemaphoreType.REGULAR,
            pltpu.SemaphoreType.REGULAR,
        ],
        compiler_params=pltpu.CompilerParams(
            collective_id=0, has_side_effects=True, vmem_limit_bytes=54 * 1024 * 1024
        ),
        cost_estimate=pl.CostEstimate(flops=13_000_000_000, bytes_accessed=25_000_000, transcendentals=1_000_000),
        name="exchange",
    )(queries, passages, neg_table, neg_ids.T, counts.reshape(1, qd), neg_home.reshape(-1, 128))
    grad_p, grad_q, loss = pl.pallas_call(
        write_kernel,
        out_shape=(
            jax.ShapeDtypeStruct((pd, d), BF16),
            jax.ShapeDtypeStruct((qd, d), BF16),
            jax.ShapeDtypeStruct((1, qd), F32),
        ),
        in_specs=[any_spec] * 3,
        out_specs=(any_spec, any_spec, any_spec),
        scratch_shapes=[dma((6,))],
        compiler_params=pltpu.CompilerParams(vmem_limit_bytes=1024 * 1024),
        cost_estimate=pl.CostEstimate(flops=0, bytes_accessed=7_300_000, transcendentals=0),
        name="write",
    )(grad_p, grad_q, loss)
    return loss.reshape(qd), grad_q, grad_p


def solution(mesh):
    in_specs = (
        P(("dp", "blk"), None),
        P(("dp", "blk"), None),
        P("dp", None),
        P(("dp", "blk"), None),
        P(("dp", "blk")),
        P(),
    )
    out_specs = (P(("dp", "blk")), P(("dp", "blk"), None), P(("dp", "blk"), None))
    return jax.shard_map(
        functools.partial(per_device, mesh.shape["dp"]),
        mesh=mesh, in_specs=in_specs, out_specs=out_specs, check_vma=False,
    )
```
